512 devices in a mesh: date: 64 (over y, x, core), pix: 8 (over z).
Axes of the slice: x: 4, y: 8, z: 8, core: 2. Of those that a mesh axis runs over, the one named last changes fastest.
Arguments:
- scene_groups: bfloat16 [512, 64, 4, 2, 16, 128], P(('date', 'pix')), may hold values from -12 to 12
- epoch_interpolator_weights: float32 [512, 8], P(('date', 'pix')), may hold values from -2.4 to 2.4
- epoch_group_numbers: int32 [512, 64], P(('date', 'pix')), may hold values from 0 to 4, as said below
- group_patch_places: int32 [512, 64, 4], P(('date', 'pix')), may hold values from 0 to 7, as said below
- epoch_couples: int32 [1200, 2], replicated, may hold values from 0 to 511, as said below
Outputs:
- displacement: float32 [512, 262144], P(None, ('date', 'pix'))
The draws below stay inside these ranges and needn't reach their ends.
Inputs may be any that keep to these rules, and one draw needn't show every extreme that they name: `epoch_group_numbers`: a date holds 4 blocks for some tiles in every draw. `group_patch_places`: the 4 entries of one date and tile are distinct slots; entries at or beyond the count are not used. epoch_couples[k, 0] < epoch_couples[k, 1] <= epoch_couples[k, 0] + 8; some pair spans 8 dates and ends at the last date.
All inputs are finite; a program needn't handle non-finite values.
Results may differ from the reference program's by a relative error of at most 0.0073.
Values may be sent and summed in bfloat16 or wider, within the bound.
A program may use at most 128 MiB of HBM per device.

```python
import jax
import jax.numpy as jnp
from jax import lax

ALONG_TRACK_LINES = 128
LOOKS = 4
TAPS = 8
PEAK_PATCH_GROUPS = 4
SLOTS = 8
SPAN = 8
PAIRS = 1200
EPOCH_TOTAL = 512
MASTER_PATCHES = 64
SLANT_BINS = 16
N_PIX = 8


def draw_epoch_group_numbers(key, part):
    key = jax.random.fold_in(key, 11)
    base_count = jax.random.randint(key, (EPOCH_TOTAL, MASTER_PATCHES), 0, PEAK_PATCH_GROUPS + 1)
    tile_load = jax.random.randint(jax.random.fold_in(key, 5), (MASTER_PATCHES,), 0, 3)
    group_totals = jnp.minimum(base_count + tile_load[None, :], PEAK_PATCH_GROUPS)
    date_index = jnp.arange(EPOCH_TOTAL, dtype=jnp.int32)[:, None]
    tile_index = jnp.arange(MASTER_PATCHES, dtype=jnp.int32)[None, :]
    group_totals = jnp.where((date_index + tile_index) % 5 == 0, PEAK_PATCH_GROUPS, group_totals)
    return group_totals.astype(jnp.int32)


def draw_group_patch_places(key, part):
    key = jax.random.fold_in(key, 23)
    scores = jax.random.randint(key, (EPOCH_TOTAL, MASTER_PATCHES, SLOTS), 0, 2 ** 20) * SLOTS + jnp.arange(SLOTS, dtype=jnp.int32)[None, None, :]
    slot_order = jnp.argsort(scores, axis=-1)
    return slot_order[:, :, :PEAK_PATCH_GROUPS].astype(jnp.int32)


def draw_epoch_couples(key, part):
    key = jax.random.fold_in(key, 37)
    first_date = jax.random.randint(key, (PAIRS,), 0, EPOCH_TOTAL - 1)
    max_gap = jnp.minimum(EPOCH_TOTAL - 1 - first_date, SPAN)
    date_gap = jax.random.randint(jax.random.fold_in(key, 3), (PAIRS,), 1, max_gap + 1)
    second_date = first_date + date_gap
    first_date = first_date.at[0].set(EPOCH_TOTAL - 1 - SPAN)
    second_date = second_date.at[0].set(EPOCH_TOTAL - 1)
    return jnp.stack([first_date, second_date], axis=1).astype(jnp.int32)


def steps_of(key, shape, split, least, largest):
    factor_of, own = 1.0, jax.random.fold_in(key, 6)
    for axis_at, shards_of in split:
        heights = jnp.exp(jax.random.uniform(jax.random.fold_in(own, axis_at), (shards_of,), jnp.float32, least / len(split), largest / len(split)))
        factor_of = factor_of * jnp.repeat(heights, shape[axis_at] // shards_of).reshape([-1 if axis == axis_at else 1 for axis in range(len(shape))])
    return factor_of


def gaussian(rng, shape, deviation, bound, pieces=(), kind=jnp.bfloat16):
    values = jax.random.normal(rng, shape, jnp.float32) * deviation
    if len(pieces) > 0:
        values = steps_of(rng, shape, pieces, -0.22, 0.18) * values
    return jnp.clip(values, min=-bound, max=bound).astype(kind)


def setup_inputs(seed: int = 0) -> dict:
    splits = jax.random.split(jax.random.key(seed), 6)
    scene_groups = gaussian(splits[0], (EPOCH_TOTAL, MASTER_PATCHES, PEAK_PATCH_GROUPS, 2, SLANT_BINS, ALONG_TRACK_LINES), 2.0, 12.0, ((0, 512),))
    epoch_interpolator_weights = gaussian(splits[1], (EPOCH_TOTAL, TAPS), 0.4, 2.4, ((0, 512),), jnp.float32)
    epoch_group_numbers = draw_epoch_group_numbers(jax.random.fold_in(splits[5], 71), 0)
    group_patch_places = draw_group_patch_places(jax.random.fold_in(splits[5], 71), 0)
    epoch_couples = draw_epoch_couples(jax.random.fold_in(splits[5], 71), 0)
    return {"scene_groups": scene_groups, "epoch_interpolator_weights": epoch_interpolator_weights, "epoch_group_numbers": epoch_group_numbers, "group_patch_places": group_patch_places, "epoch_couples": epoch_couples}


damping = 1.0
pair_block = 400

def row_kernels(epoch_filter_weights):
    rows_in = jnp.arange(ALONG_TRACK_LINES, dtype=jnp.int32)[:, None]
    rows_out = jnp.arange(ALONG_TRACK_LINES, dtype=jnp.int32)[None, :]
    row_lag = rows_in - rows_out + TAPS // 2
    kernel = jnp.zeros((epoch_filter_weights.shape[0], ALONG_TRACK_LINES, ALONG_TRACK_LINES), jnp.float32)
    for tap_index in range(TAPS):
        chosen = jnp.where(row_lag == tap_index, 1.0, 0.0).astype(jnp.float32)
        kernel = kernel + chosen[None] * epoch_filter_weights[:, tap_index][:, None, None]
    return kernel.astype(jnp.bfloat16)

def arrange_groups(scene_pixel_values, group_totals, place_indices):
    in_use = jnp.arange(PEAK_PATCH_GROUPS, dtype=jnp.int32)[None, None, :] < group_totals[:, :, None]
    place_chooser = jnp.logical_and(place_indices[..., None] == jnp.arange(SLOTS, dtype=jnp.int32)[None, None, None, :], in_use[..., None])
    place_chooser = place_chooser.astype(jnp.float32)
    arranged_groups = jnp.einsum('ukijam,ukis->uksjam', scene_pixel_values.astype(jnp.float32), place_chooser, precision=lax.Precision.HIGHEST)
    return arranged_groups.astype(jnp.bfloat16)

def prepared_epoch_groups(epoch_inputs):
    epoch_scene_groups, epoch_filter_weights, group_totals, place_indices = epoch_inputs
    arranged_groups = arrange_groups(epoch_scene_groups[None], group_totals[None], place_indices[None])
    kernel = row_kernels(epoch_filter_weights[None])
    interpolated_groups = jnp.einsum('ntsxyr,nrq->ntsxyq', arranged_groups.astype(jnp.float32), kernel.astype(jnp.float32), precision=lax.Precision.HIGHEST)
    return interpolated_groups[0].astype(jnp.bfloat16)

def pair_phase(tile_stack, first_date, second_date):
    earlier_slc = jnp.take(tile_stack, first_date, axis=0).astype(jnp.float32)
    later_slc = jnp.take(tile_stack, second_date, axis=0).astype(jnp.float32)
    real_part = earlier_slc[:, :, 0] * later_slc[:, :, 0] + earlier_slc[:, :, 1] * later_slc[:, :, 1]
    imag_part = earlier_slc[:, :, 1] * later_slc[:, :, 0] - earlier_slc[:, :, 0] * later_slc[:, :, 1]
    look_shape = real_part.shape[:-1] + (ALONG_TRACK_LINES // LOOKS, LOOKS)
    real_part = lax.optimization_barrier(jnp.sum(real_part.reshape(look_shape), axis=-1)) * (1.0 / LOOKS)
    imag_part = lax.optimization_barrier(jnp.sum(imag_part.reshape(look_shape), axis=-1)) * (1.0 / LOOKS)
    return imag_part / jnp.sqrt(jnp.maximum(real_part * real_part + imag_part * imag_part, 1.0))

def all_phases(tile_stack, epoch_couples):
    blocked = epoch_couples.reshape(PAIRS // pair_block, pair_block, 2)

    def one_block(pair_rows):
        return pair_phase(tile_stack, pair_rows[:, 0], pair_rows[:, 1])
    phases = lax.map(one_block, blocked)
    return phases.reshape((PAIRS,) + phases.shape[2:])

def invert_pairs(factor, design, phases):
    right = jnp.dot(design, phases, precision=lax.Precision.HIGHEST)
    middle = lax.linalg.triangular_solve(factor, right, left_side=True, lower=True, transpose_a=False)
    return lax.linalg.triangular_solve(factor, middle, left_side=True, lower=True, transpose_a=True)

def normal_matrix(epoch_couples, total_dates):
    earlier = epoch_couples[:, 0]
    later = epoch_couples[:, 1]
    normal_system = damping * jnp.eye(total_dates, dtype=jnp.float32)
    normal_system = normal_system.at[later, later].add(1.0)
    normal_system = normal_system.at[earlier, earlier].add(1.0)
    normal_system = normal_system.at[earlier, later].add(-1.0)
    normal_system = normal_system.at[later, earlier].add(-1.0)
    return normal_system

def build_design(epoch_couples):
    dates_column = jnp.arange(EPOCH_TOTAL, dtype=jnp.int32)[:, None]
    later_hit = (epoch_couples[:, 1][None, :] == dates_column).astype(jnp.float32)
    earlier_hit = (epoch_couples[:, 0][None, :] == dates_column).astype(jnp.float32)
    design = later_hit - earlier_hit
    normal_system = normal_matrix(epoch_couples, EPOCH_TOTAL)
    return (design, jnp.linalg.cholesky(normal_system))

def reference(scene_groups, epoch_interpolator_weights, epoch_group_numbers, group_patch_places, epoch_couples):
    interpolated_groups = lax.map(prepared_epoch_groups, (scene_groups, epoch_interpolator_weights, epoch_group_numbers, group_patch_places))
    design, factor = build_design(epoch_couples)
    col_dev = SLANT_BINS // N_PIX

    def tile_solve(tile_index):
        tile_stack = lax.dynamic_index_in_dim(interpolated_groups, tile_index, 1, keepdims=False)
        phases = all_phases(tile_stack, epoch_couples)
        phases = phases.reshape(PAIRS, SLOTS, N_PIX, col_dev, ALONG_TRACK_LINES // LOOKS)
        phases = phases.transpose(0, 2, 1, 3, 4).reshape(PAIRS, -1)
        return invert_pairs(factor, design, phases)
    solved = lax.map(tile_solve, jnp.arange(MASTER_PATCHES, dtype=jnp.int32))
    return solved.transpose(1, 0, 2).reshape(EPOCH_TOTAL, -1)
```

```python
import jax
import jax.numpy as jnp
from jax import lax
from jax.experimental import pallas as pl
from jax.experimental.pallas import tpu as pltpu
from jax.sharding import PartitionSpec as P

ALONG_TRACK_LINES = 128
LOOKS = 4
TAPS = 8
GROUPS = 4
SLOTS = 8
PAIRS = 1200
DATES = 512
HALF = 608
PADDED = 2 * HALF
BLOCKS = 64
TILES = 64
HALF_TILES = 32
N_PIX = 8
CHUNK = 8
BATCH = 16
EARLY_LEVELS = 3
VMEM_BYTES = 56 * 1024 * 1024
MESH = pl.DeviceIdType.MESH
f32 = jnp.float32
bf16 = jnp.bfloat16
HIGHEST = lax.Precision.HIGHEST


def iota(shape, dim):
    return lax.broadcasted_iota(jnp.int32, shape, dim)


def dot(a, b):
    return jnp.dot(a, b, preferred_element_type=f32)


def split2(x):
    high = x.astype(bf16)
    low = (x - high.astype(f32)).astype(bf16)
    return high, low


def build_row_matrix(w_ref, e_ref):
    lane = iota((128, 128), 1)
    lag = iota((128, 128), 0) - 4 * (lane % 32) + TAPS // 2
    for j in range(LOOKS):
        taps = jnp.zeros((128, 128), f32)
        for tap in range(TAPS):
            taps = jnp.where(lag - j == tap, w_ref[0, tap], taps)
        for g in range(4):
            e_ref[g * 128 : (g + 1) * 128, j * 128 : (j + 1) * 128] = jnp.where(
                lane // 32 == g, taps, 0.0
            ).astype(bf16)


def resample(x_ref, w_ref, e_ref, spread_ref, o_ref):
    build_row_matrix(w_ref, e_ref)
    row = iota((128, 128), 0)
    column = iota((128, 128), 1)
    source = (row % 4) * 32 + (row // 64) * 16 + (row // 4 % 8) * 2 + row // 32 % 2
    pick = jnp.where(source == column, 1.0, 0.0).astype(bf16)

    def one_chunk(step, carry):
        parts = []
        for k in range(CHUNK):
            at = pl.multiple_of((step * CHUNK + k) * 128, 128)
            g = dot(pick, x_ref[pl.ds(at, 128), :]).astype(bf16)
            parts.append(
                jnp.concatenate([g[32 * q : 32 * (q + 1)] for q in range(4)], axis=1)
            )
        lhs = jnp.concatenate(parts, axis=0)
        y = dot(lhs, e_ref[...])
        rows = CHUNK * 32
        for j in range(LOOKS):
            spread_ref[pl.ds(j, rows, stride=LOOKS), :] = y[:, j * 128 : (j + 1) * 128]
        for k in range(CHUNK // 2):
            u = step * (CHUNK // 2) + k
            o_ref[u] = (
                spread_ref[k * 256 : (k + 1) * 256, :].astype(bf16).reshape(2, 8, 16, 128)
            )
        return carry

    lax.fori_loop(0, TILES // CHUNK, one_chunk, 0)


def block_inverse(rows):
    sub = iota((8, 128), 0)
    rows = list(rows)
    for k in range(8):
        inverse = 1.0 / rows[k][k : k + 1, :]
        pivot = jnp.where(sub == k, inverse, rows[k] * inverse)
        for r in range(8):
            if r != k:
                rows[r] = jnp.where(sub == k, 0.0, rows[r]) - rows[r][k : k + 1, :] * pivot
        rows[k] = pivot
    return rows


def block_product(a, b):
    out = []
    for r in range(8):
        total = a[r][0:1, :] * b[0]
        for k in range(1, 8):
            total = total + a[r][k : k + 1, :] * b[k]
        out.append(total)
    return out


def shifted(rows, amount):
    return [pltpu.roll(x, amount, 1) for x in rows]


def joined(rows):
    lane = iota((8, 128), 1)
    return jnp.concatenate(
        [
            jnp.where(lane < 64, rows[2 * q], pltpu.roll(rows[2 * q + 1], 64, 1))
            for q in range(4)
        ],
        axis=1,
    )


def normal_parts(couples_ref, design_ref):
    position = iota((DATES, PADDED), 0)
    date = (position % BLOCKS) * 8 + position // BLOCKS
    later = jnp.where(date == couples_ref[1:2, :], 1.0, 0.0)
    earlier = jnp.where(date == couples_ref[0:1, :], 1.0, 0.0)
    design_ref[...] = (later - earlier).astype(bf16)
    lane = iota((BLOCKS, 512), 1)
    offset = iota((BLOCKS, 512), 0) - lane % BLOCKS
    parts = {-1: [], 0: [], 1: []}
    for c in range(8):
        rows = lax.dot_general(
            design_ref[c * 64 : (c + 1) * 64, :],
            design_ref[...],
            (((1,), (1,)), ((), ())),
            preferred_element_type=f32,
        )
        rows = rows + jnp.where((offset == 0) & (lane // BLOCKS == c), 1.0, 0.0)
        for at in parts:
            parts[at].append(
                jnp.sum(jnp.where(offset == at, rows, 0.0), axis=0, keepdims=True)
            )
    small = iota((8, 128), 1)
    sub = iota((8, 128), 0)
    out = []
    for at in (-1, 0, 1):
        whole = jnp.concatenate(parts[at], axis=0)
        rows = []
        for r in range(8):
            x = whole[:, (r // 2) * 128 : (r // 2 + 1) * 128]
            if r % 2:
                x = pltpu.roll(x, 64, 1)
            pad = jnp.where(sub == r, 1.0, 0.0) if at == 0 else jnp.zeros((8, 128), f32)
            rows.append(jnp.where(small < 64, x, pad))
        out.append(tuple(rows))
    return tuple(out)


def write_factor(factor_ref, before, at, after, hop):
    lane = iota((BLOCKS, 512), 1)
    offset = iota((BLOCKS, 512), 0) - lane % BLOCKS
    for c in range(8):
        x = jnp.where(offset == 0, at[c : c + 1, :], 0.0)
        if before is not None:
            x = jnp.where(offset == -hop, before[c : c + 1, :], x)
            x = jnp.where(offset == hop, after[c : c + 1, :], x)
        factor_ref[c * 64 : (c + 1) * 64, :] = x


def times_factor(left_ref, factor_ref):
    def one_block(step, carry):
        at = pl.multiple_of(step * 128, 128)
        rows = pl.ds(at, 128)
        left_ref[rows, :] = jnp.dot(
            left_ref[rows, :], factor_ref[...], preferred_element_type=f32, precision=HIGHEST
        )
        return carry

    lax.fori_loop(0, 4, one_block, 0)


def reduce_levels(parts, left_ref, factor_ref, levels, first):
    lane512 = iota((8, 512), 1)
    unit = jnp.where(iota((8, 512), 0) == lane512 // BLOCKS, 1.0, 0.0)

    def one_level(level, carry):
        low, mid, up = carry
        hop = jnp.left_shift(1, level)
        back = 128 - hop
        inverse = block_inverse(mid)
        alpha = [-x for x in block_product(low, shifted(inverse, hop))]
        gamma = [-x for x in block_product(up, shifted(inverse, back))]
        write_factor(factor_ref, joined(alpha), unit, joined(gamma), hop)
        add_low = block_product(alpha, shifted(up, hop))
        add_up = block_product(gamma, shifted(low, back))
        mid = tuple(m + a + b for m, a, b in zip(mid, add_low, add_up))
        new_low = tuple(block_product(alpha, shifted(low, hop)))
        new_up = tuple(block_product(gamma, shifted(up, back)))
        times_factor(left_ref, factor_ref)
        return new_low, mid, new_up

    return lax.fori_loop(first, first + levels, one_level, parts)


def start_left(left_ref):
    left_ref[...] = jnp.where(
        iota((DATES, DATES), 0) == iota((DATES, DATES), 1), 1.0, 0.0
    )


def finish_operator(parts, left_ref, factor_ref, terms_ref, design_ref, high_ref, low_ref):
    inverse = joined(block_inverse(parts[1]))
    write_factor(factor_ref, None, inverse, None, 0)
    times_factor(left_ref, factor_ref)
    x = left_ref[...]
    x1, x2 = split2(x)
    terms_ref[0] = x1
    terms_ref[1] = x2
    terms_ref[2] = (x - x1.astype(f32) - x2.astype(f32)).astype(bf16)

    def one_block(step, carry):
        at = pl.multiple_of(step * 128, 128)
        date = iota((128, DATES), 0) + at
        position = iota((128, DATES), 1)
        order = jnp.where(
            (position % BLOCKS) * 8 + position // BLOCKS == date, 1.0, 0.0
        ).astype(bf16)
        m = jnp.zeros((128, PADDED), f32)
        for term in (2, 1, 0):
            m = m + dot(dot(order, terms_ref[term]).astype(bf16), design_ref[...])
        high, low = split2(m)
        high_ref[pl.ds(at, 128), :] = high
        low_ref[pl.ds(at, 128), :] = low
        return carry

    lax.fori_loop(0, DATES // 128, one_block, 0)


def exchange_kernel(
    x_ref, w_ref, couples_ref, own_codes_ref,
    landed_ref, high_ref, low_ref, codes_ref,
    c_mid, c_sum, c_all,
    e_ref, spread_ref, o_ref, z_mid, d_mid, design_ref, left_ref, factor_ref, terms_ref,
    send_z1, recv_z1, send_d1, recv_d1, send_d2, recv_d2, send_z2, recv_z2, local_sem,
    send_c1, recv_c1, send_c2, recv_c2,
):
    a = lax.axis_index("date")
    z = lax.axis_index("pix")
    core = lax.rem(a, 2)
    other = 1 - core
    u = lax.div(a, 2)

    def z_of(step):
        return lax.rem(z + step, N_PIX)

    def u_of(step):
        return lax.rem(u + step, HALF_TILES)

    barrier = pltpu.get_barrier_semaphore()

    def greet(device):
        pl.semaphore_signal(barrier, inc=1, device_id=device, device_id_type=MESH)

    def greet_pix(step, carry):
        greet((a, z_of(step)))
        return carry

    def greet_same(step, carry):
        greet((2 * u_of(step) + core, z))
        return carry

    def greet_other(step, carry):
        greet((2 * u_of(step) + other, z))
        return carry

    lax.fori_loop(1, N_PIX, greet_pix, 0)
    lax.fori_loop(1, HALF_TILES, greet_same, 0)
    lax.fori_loop(0, HALF_TILES, greet_other, 0)

    resample(x_ref, w_ref, e_ref, spread_ref, o_ref)

    pl.semaphore_wait(barrier, N_PIX - 1 + HALF_TILES - 1 + HALF_TILES)

    def pix_first(step):
        to = z_of(step)
        return pltpu.make_async_remote_copy(
            src_ref=o_ref.at[:, core, to], dst_ref=z_mid.at[z],
            send_sem=send_z1.at[step], recv_sem=recv_z1.at[step],
            device_id=(a, to), device_id_type=MESH,
        )

    def date_first(step):
        to = u_of(step)
        return pltpu.make_async_remote_copy(
            src_ref=o_ref.at[to, other], dst_ref=d_mid.at[u],
            send_sem=send_d1.at[step], recv_sem=recv_d1.at[step],
            device_id=(2 * to + other, z), device_id_type=MESH,
        )

    def date_second(step):
        to = u_of(step)
        return pltpu.make_async_remote_copy(
            src_ref=z_mid.at[:, to], dst_ref=landed_ref.at[u, core],
            send_sem=send_d2.at[step], recv_sem=recv_d2.at[step],
            device_id=(2 * to + core, z), device_id_type=MESH,
        )

    def pix_second(step):
        to = z_of(step)
        return pltpu.make_async_remote_copy(
            src_ref=d_mid.at[:, to], dst_ref=landed_ref.at[:, other, z],
            send_sem=send_z2.at[step], recv_sem=recv_z2.at[step],
            device_id=(a, to), device_id_type=MESH,
        )

    def arrival_pix_first(step):
        at = lax.rem(z + N_PIX - step, N_PIX)
        return pltpu.make_async_remote_copy(
            src_ref=o_ref.at[:, core, at], dst_ref=z_mid.at[at],
            send_sem=send_z1.at[step], recv_sem=recv_z1.at[step],
            device_id=(a, at), device_id_type=MESH,
        )

    def arrival_date_first(step):
        at = lax.rem(u + HALF_TILES - step, HALF_TILES)
        return pltpu.make_async_remote_copy(
            src_ref=o_ref.at[at, other], dst_ref=d_mid.at[at],
            send_sem=send_d1.at[step], recv_sem=recv_d1.at[step],
            device_id=(2 * at + other, z), device_id_type=MESH,
        )

    def arrival_date_second(step):
        at = lax.rem(u + HALF_TILES - step, HALF_TILES)
        return pltpu.make_async_remote_copy(
            src_ref=z_mid.at[:, at], dst_ref=landed_ref.at[at, core],
            send_sem=send_d2.at[step], recv_sem=recv_d2.at[step],
            device_id=(2 * at + core, z), device_id_type=MESH,
        )

    def arrival_pix_second(step):
        at = lax.rem(z + N_PIX - step, N_PIX)
        return pltpu.make_async_remote_copy(
            src_ref=d_mid.at[:, at], dst_ref=landed_ref.at[:, other, at],
            send_sem=send_z2.at[step], recv_sem=recv_z2.at[step],
            device_id=(a, at), device_id_type=MESH,
        )

    def code_to_other(step):
        to = 2 * u_of(step) + other
        return pltpu.make_async_remote_copy(
            src_ref=own_codes_ref.at[to], dst_ref=c_mid.at[a],
            send_sem=send_c1.at[step], recv_sem=recv_c1.at[step],
            device_id=(to, z), device_id_type=MESH,
        )

    def code_to_same(step):
        to = 2 * u_of(step) + core
        return pltpu.make_async_remote_copy(
            src_ref=own_codes_ref.at[to], dst_ref=c_mid.at[a],
            send_sem=send_c1.at[HALF_TILES + step], recv_sem=recv_c1.at[HALF_TILES + step],
            device_id=(to, z), device_id_type=MESH,
        )

    def arrival_code_other(step):
        at = 2 * lax.rem(u + HALF_TILES - step, HALF_TILES) + other
        return pltpu.make_async_remote_copy(
            src_ref=own_codes_ref.at[at], dst_ref=c_mid.at[at],
            send_sem=send_c1.at[step], recv_sem=recv_c1.at[step],
            device_id=(at, z), device_id_type=MESH,
        )

    def arrival_code_same(step):
        at = 2 * lax.rem(u + HALF_TILES - step, HALF_TILES) + core
        return pltpu.make_async_remote_copy(
            src_ref=own_codes_ref.at[at], dst_ref=c_mid.at[at],
            send_sem=send_c1.at[HALF_TILES + step], recv_sem=recv_c1.at[HALF_TILES + step],
            device_id=(at, z), device_id_type=MESH,
        )

    def code_second(step):
        to = z_of(step)
        return pltpu.make_async_remote_copy(
            src_ref=c_sum, dst_ref=c_all.at[z],
            send_sem=send_c2.at[step], recv_sem=recv_c2.at[step],
            device_id=(a, to), device_id_type=MESH,
        )

    def arrival_code_second(step):
        at = lax.rem(z + N_PIX - step, N_PIX)
        return pltpu.make_async_remote_copy(
            src_ref=c_sum, dst_ref=c_all.at[at],
            send_sem=send_c2.at[step], recv_sem=recv_c2.at[step],
            device_id=(a, at), device_id_type=MESH,
        )

    def each(first, last, act):
        def body(step, carry):
            act(step)
            return carry

        lax.fori_loop(first, last, body, 0)

    each(1, N_PIX, lambda s: pix_first(s).start())
    each(0, HALF_TILES, lambda s: date_first(s).start())
    own_first = pltpu.make_async_copy(o_ref.at[:, core, z], z_mid.at[z], local_sem.at[0])
    own_first.start()
    each(0, HALF_TILES, lambda s: code_to_other(s).start())
    each(1, HALF_TILES, lambda s: code_to_same(s).start())
    c_mid[a] = own_codes_ref[a]

    parts = normal_parts(couples_ref, design_ref)
    start_left(left_ref)
    parts = reduce_levels(parts, left_ref, factor_ref, EARLY_LEVELS, 0)

    each(0, HALF_TILES, lambda s: arrival_code_other(s).wait_recv())
    each(1, HALF_TILES, lambda s: arrival_code_same(s).wait_recv())
    for p in range(8):
        c_sum[p : p + 1, :] = jnp.sum(c_mid[8 * p : 8 * (p + 1)], axis=0)
    c_all[z] = c_sum[...]
    each(1, N_PIX, lambda s: code_second(s).start())

    own_first.wait()
    each(1, N_PIX, lambda s: arrival_pix_first(s).wait_recv())
    each(1, HALF_TILES, lambda s: date_second(s).start())
    own_date = pltpu.make_async_copy(
        z_mid.at[:, u], landed_ref.at[u, core], local_sem.at[1]
    )
    own_date.start()
    each(0, HALF_TILES, lambda s: arrival_date_first(s).wait_recv())
    each(1, N_PIX, lambda s: pix_second(s).start())
    own_pix = pltpu.make_async_copy(
        d_mid.at[:, z], landed_ref.at[:, other, z], local_sem.at[2]
    )
    own_pix.start()

    parts = reduce_levels(parts, left_ref, factor_ref, 6 - EARLY_LEVELS, EARLY_LEVELS)
    finish_operator(parts, left_ref, factor_ref, terms_ref, design_ref, high_ref, low_ref)

    own_date.wait()
    own_pix.wait()
    each(1, HALF_TILES, lambda s: arrival_date_second(s).wait_recv())
    each(1, N_PIX, lambda s: arrival_pix_second(s).wait_recv())
    each(1, N_PIX, lambda s: arrival_code_second(s).wait_recv())
    codes_ref[...] = c_all[...]
    each(0, HALF_TILES, lambda s: code_to_other(s).wait_send())
    each(1, HALF_TILES, lambda s: code_to_same(s).wait_send())
    each(1, N_PIX, lambda s: code_second(s).wait_send())
    each(1, N_PIX, lambda s: pix_first(s).wait_send())
    each(0, HALF_TILES, lambda s: date_first(s).wait_send())
    each(1, HALF_TILES, lambda s: date_second(s).wait_send())
    each(1, N_PIX, lambda s: pix_second(s).wait_send())


def exchange(x, w, couples, own_codes):
    vmem = pl.BlockSpec(memory_space=pltpu.VMEM)
    dma = pltpu.SemaphoreType.DMA
    return pl.pallas_call(
        exchange_kernel,
        out_shape=(
            jax.ShapeDtypeStruct((HALF_TILES, 2, N_PIX, 16, 128), bf16),
            jax.ShapeDtypeStruct((DATES, PADDED), bf16),
            jax.ShapeDtypeStruct((DATES, PADDED), bf16),
            jax.ShapeDtypeStruct((N_PIX, 8, 128), f32),
        ),
        in_specs=[vmem, pl.BlockSpec(memory_space=pltpu.SMEM), vmem, vmem],
        out_specs=(pl.BlockSpec(memory_space=pl.ANY), vmem, vmem, vmem),
        scratch_shapes=[
            pltpu.VMEM((TILES, 1, 128), f32),
            pltpu.VMEM((8, 128), f32),
            pltpu.VMEM((N_PIX, 8, 128), f32),
            pltpu.VMEM((512, 512), bf16),
            pltpu.VMEM((CHUNK * 128, 128), f32),
            pltpu.VMEM((HALF_TILES, 2, N_PIX, 16, 128), bf16),
            pltpu.VMEM((N_PIX, HALF_TILES, 16, 128), bf16),
            pltpu.VMEM((HALF_TILES, N_PIX, 16, 128), bf16),
            pltpu.VMEM((DATES, PADDED), bf16),
            pltpu.VMEM((DATES, DATES), f32),
            pltpu.VMEM((DATES, DATES), f32),
            pltpu.VMEM((3, DATES, DATES), bf16),
            dma((N_PIX,)), dma((N_PIX,)),
            dma((HALF_TILES,)), dma((HALF_TILES,)),
            dma((HALF_TILES,)), dma((HALF_TILES,)),
            dma((N_PIX,)), dma((N_PIX,)),
            dma((3,)),
            dma((2 * HALF_TILES,)), dma((2 * HALF_TILES,)),
            dma((N_PIX,)), dma((N_PIX,)),
        ],
        compiler_params=pltpu.CompilerParams(
            collective_id=0, has_side_effects=True, vmem_limit_bytes=VMEM_BYTES
        ),
        name="exchange",
    )(x, w, couples, own_codes)


def phase_kernel(
    landed_ref, codes_ref, high_ref, low_ref, couples_ref, out_ref,
    stack_ref, swapped_ref, phase_ref,
):
    row = iota((256, 128), 0)
    column = iota((256, 128), 1)
    fits = (row // 32 == column // 16) & (row // 8 % 4 == column % 4)
    slot = jnp.where(fits, row % 8, -1).astype(f32)
    half = iota((128, 128), 1) < 64

    def place(group, carry):
        pix = lax.div(group, 8)
        eighth = lax.rem(group, 8)
        blocks = landed_ref[pl.ds(eighth * 8, 8), pix].reshape(128, 128)
        chooser = jnp.where(slot == codes_ref[pl.ds(group, 1), :], 1.0, 0.0).astype(bf16)
        turned = pltpu.roll(blocks.astype(f32), 64, 1)
        turned = jnp.where(half, -turned, turned).astype(bf16)
        placed = dot(chooser, jnp.concatenate([blocks, turned], axis=1))
        for q in range(8):
            to = pl.ds(pl.multiple_of(((eighth * 8 + q) * 8 + pix) * 32, 32), 32)
            stack_ref[to, :] = placed[q * 32 : (q + 1) * 32, :128]
            swapped_ref[to, :] = placed[q * 32 : (q + 1) * 32, 128:]
        return carry

    lax.fori_loop(0, BLOCKS, place, 0, unroll=8)

    low_half = iota((8, 128), 1) < 64

    def one_pair(k):
        first = pl.multiple_of(couples_ref[0, k] * 32, 32)
        second = pl.multiple_of(couples_ref[1, k] * 32, 32)
        real = imag = None
        for j in range(LOOKS):
            earlier = stack_ref[pl.ds(first + 8 * j, 8), :]
            r = earlier * stack_ref[pl.ds(second + 8 * j, 8), :]
            i = earlier * swapped_ref[pl.ds(second + 8 * j, 8), :]
            real = r if real is None else real + r
            imag = i if imag is None else imag + i
        return real, imag

    def merge(v, w):
        return jnp.where(low_half, v, w) + pltpu.roll(jnp.where(low_half, w, v), 64, 1)

    def pairs(step, carry):
        found = [
            (one_pair(step * BATCH + q), one_pair(step * BATCH + q + HALF))
            for q in range(BATCH)
        ]
        phases = []
        for (r0, i0), (r1, i1) in found:
            real = merge(r0, r1)
            imag = merge(i0, i1)
            power = jnp.maximum(real * real + imag * imag, float(LOOKS * LOOKS))
            phases.append(imag * lax.rsqrt(power))
        to = pl.ds(pl.multiple_of(step * (8 * BATCH), 8 * BATCH), 8 * BATCH)
        phase_ref[to, :] = jnp.concatenate(phases, axis=0)
        return carry

    lax.fori_loop(0, HALF // BATCH, pairs, 0)

    wide = iota((HALF, 128), 1) < 64
    for part in range(2):
        columns = []
        for p in (2 * part, 2 * part + 1):
            a0 = phase_ref[pl.ds(2 * p, HALF, stride=8), :]
            a1 = phase_ref[pl.ds(2 * p + 1, HALF, stride=8), :]
            columns.append(
                jnp.concatenate(
                    [
                        jnp.where(wide, a0, pltpu.roll(a1, 64, 1)),
                        jnp.where(wide, pltpu.roll(a0, 64, 1), a1),
                    ],
                    axis=0,
                )
            )
        high, low = split2(jnp.concatenate(columns, axis=1))
        out_ref[:, part * 256 : (part + 1) * 256] = dot(high_ref[...], high) + (
            dot(high_ref[...], low) + dot(low_ref[...], high)
        )


def solve_phases(landed, codes, high, low, couples):
    vmem = pl.BlockSpec(memory_space=pltpu.VMEM)
    return pl.pallas_call(
        phase_kernel,
        out_shape=jax.ShapeDtypeStruct((DATES, 512), f32),
        in_specs=[vmem, vmem, vmem, vmem, pl.BlockSpec(memory_space=pltpu.SMEM)],
        out_specs=vmem,
        scratch_shapes=[
            pltpu.VMEM((DATES * 32, 128), f32),
            pltpu.VMEM((DATES * 32, 128), f32),
            pltpu.VMEM((HALF * 8, 128), f32),
        ],
        compiler_params=pltpu.CompilerParams(vmem_limit_bytes=VMEM_BYTES),
        name="phases",
    )(landed, codes, high, low, couples)


def local(scene_groups, weights, numbers, places, couples):
    in_use = jnp.arange(GROUPS, dtype=jnp.int32)[None, :] < numbers[0][:, None]
    codes = jnp.where(in_use, places[0], SLOTS).astype(bf16)
    group = jnp.arange(GROUPS, dtype=jnp.int32)[:, None]
    lane = jnp.arange(128, dtype=jnp.int32)[None, :]
    eighth = lax.rem(lax.axis_index("date"), 8)
    spread = (lane // LOOKS % GROUPS == group) & (lane // 16 == eighth)
    own_codes = jnp.dot(codes, spread.astype(bf16), preferred_element_type=f32)
    couples = jnp.pad(couples.T, ((0, 0), (0, PADDED - PAIRS)))
    landed, high, low, codes = exchange(
        scene_groups.reshape(TILES * 128, 128), weights, couples,
        own_codes.reshape(TILES, 1, 128),
    )
    return solve_phases(
        landed.reshape(TILES, N_PIX, 16, 128), codes.reshape(BLOCKS, 128), high, low, couples
    )


def solution(mesh):
    in_specs = (
        P(("date", "pix"), None, None, None, None, None),
        P(("date", "pix"), None),
        P(("date", "pix"), None),
        P(("date", "pix"), None, None),
        P(),
    )
    out_specs = P(None, ("date", "pix"))
    return jax.shard_map(local, mesh=mesh, in_specs=in_specs, out_specs=out_specs, check_vma=False)
```

```python
import jax
import jax.numpy as jnp
from jax import lax
from jax.experimental import pallas as pl
from jax.experimental.pallas import tpu as pltpu
from jax.sharding import PartitionSpec as P

ALONG_TRACK_LINES = 128
LOOKS = 4
TAPS = 8
GROUPS = 4
SLOTS = 8
PAIRS = 1200
DATES = 512
HALF = PAIRS // 2
BLOCKS = 64
TILES = 64
HALF_TILES = 32
N_PIX = 8
CHUNK = 8
BATCH = 40
EARLY_LEVELS = 3
VMEM_BYTES = 56 * 1024 * 1024
MESH = pl.DeviceIdType.MESH
f32 = jnp.float32
bf16 = jnp.bfloat16
HIGHEST = lax.Precision.HIGHEST


def iota(shape, dim):
    return lax.broadcasted_iota(jnp.int32, shape, dim)


def dot(a, b):
    return jnp.dot(a, b, preferred_element_type=f32)


def split2(x):
    high = x.astype(bf16)
    low = (x - high.astype(f32)).astype(bf16)
    return high, low


def build_row_matrix(w_ref, e_ref):
    lane = iota((128, 128), 1)
    lag = iota((128, 128), 0) - 4 * (lane % 32) + TAPS // 2
    for j in range(LOOKS):
        taps = jnp.zeros((128, 128), f32)
        for tap in range(TAPS):
            taps = jnp.where(lag - j == tap, w_ref[0, tap], taps)
        for g in range(4):
            e_ref[g * 128 : (g + 1) * 128, j * 128 : (j + 1) * 128] = jnp.where(
                lane // 32 == g, taps, 0.0
            ).astype(bf16)


def resample_chunk(at, pick, x_ref, e_ref, spread_ref, o_ref):
    parts = []
    for k in range(CHUNK):
        rows = pl.ds(pl.multiple_of((at * CHUNK + k) * 128, 128), 128)
        g = dot(pick, x_ref[rows, :]).astype(bf16)
        parts.append(jnp.concatenate([g[32 * q : 32 * (q + 1)] for q in range(4)], axis=1))
    y = dot(jnp.concatenate(parts, axis=0), e_ref[...])
    for j in range(LOOKS):
        spread_ref[pl.ds(j, CHUNK * 32, stride=LOOKS), :] = y[:, j * 128 : (j + 1) * 128]
    for k in range(CHUNK // 2):
        o_ref[at * (CHUNK // 2) + k] = (
            spread_ref[k * 256 : (k + 1) * 256, :].astype(bf16).reshape(2, 8, 16, 128)
        )


def row_picker():
    row = iota((128, 128), 0)
    column = iota((128, 128), 1)
    source = (row % 4) * 32 + (row // 64) * 16 + (row // 4 % 8) * 2 + row // 32 % 2
    return jnp.where(source == column, 1.0, 0.0).astype(bf16)


def block_inverse(rows):
    sub = iota((8, 128), 0)
    rows = list(rows)
    for k in range(8):
        inverse = 1.0 / rows[k][k : k + 1, :]
        pivot = jnp.where(sub == k, inverse, rows[k] * inverse)
        for r in range(8):
            if r != k:
                rows[r] = jnp.where(sub == k, 0.0, rows[r]) - rows[r][k : k + 1, :] * pivot
        rows[k] = pivot
    return rows


def block_product(a, b):
    out = []
    for r in range(8):
        total = a[r][0:1, :] * b[0]
        for k in range(1, 8):
            total = total + a[r][k : k + 1, :] * b[k]
        out.append(total)
    return out


def shifted(rows, amount):
    return [pltpu.roll(x, amount, 1) for x in rows]


def joined(rows):
    lane = iota((8, 128), 1)
    return jnp.concatenate(
        [
            jnp.where(lane < 64, rows[2 * q], pltpu.roll(rows[2 * q + 1], 64, 1))
            for q in range(4)
        ],
        axis=1,
    )


def normal_parts(couples_ref, design_ref):
    position = iota((DATES, PAIRS), 0)
    date = (position % BLOCKS) * 8 + position // BLOCKS
    later = jnp.where(date == couples_ref[1:2, :], 1.0, 0.0)
    earlier = jnp.where(date == couples_ref[0:1, :], 1.0, 0.0)
    design_ref[...] = (later - earlier).astype(bf16)
    lane = iota((BLOCKS, 512), 1)
    offset = iota((BLOCKS, 512), 0) - lane % BLOCKS
    parts = {-1: [], 0: [], 1: []}
    for c in range(8):
        rows = lax.dot_general(
            design_ref[c * 64 : (c + 1) * 64, :],
            design_ref[...],
            (((1,), (1,)), ((), ())),
            preferred_element_type=f32,
        )
        rows = rows + jnp.where((offset == 0) & (lane // BLOCKS == c), 1.0, 0.0)
        for at in parts:
            parts[at].append(
                jnp.sum(jnp.where(offset == at, rows, 0.0), axis=0, keepdims=True)
            )
    small = iota((8, 128), 1)
    sub = iota((8, 128), 0)
    out = []
    for at in (-1, 0, 1):
        whole = jnp.concatenate(parts[at], axis=0)
        rows = []
        for r in range(8):
            x = whole[:, (r // 2) * 128 : (r // 2 + 1) * 128]
            if r % 2:
                x = pltpu.roll(x, 64, 1)
            pad = jnp.where(sub == r, 1.0, 0.0) if at == 0 else jnp.zeros((8, 128), f32)
            rows.append(jnp.where(small < 64, x, pad))
        out.append(tuple(rows))
    return tuple(out)


def write_factor(factor_ref, before, at, after, hop):
    lane = iota((BLOCKS, 512), 1)
    offset = iota((BLOCKS, 512), 0) - lane % BLOCKS
    for c in range(8):
        x = jnp.where(offset == 0, at[c : c + 1, :], 0.0)
        if before is not None:
            x = jnp.where(offset == -hop, before[c : c + 1, :], x)
            x = jnp.where(offset == hop, after[c : c + 1, :], x)
        factor_ref[c * 64 : (c + 1) * 64, :] = x


def times_factor(left_ref, factor_ref):
    def one_block(step, carry):
        at = pl.multiple_of(step * 128, 128)
        rows = pl.ds(at, 128)
        left_ref[rows, :] = jnp.dot(
            left_ref[rows, :], factor_ref[...], preferred_element_type=f32, precision=HIGHEST
        )
        return carry

    lax.fori_loop(0, 4, one_block, 0)


def reduce_level(level, parts, write_ref):
    low, mid, up = parts
    unit = jnp.where(iota((8, 512), 0) == iota((8, 512), 1) // BLOCKS, 1.0, 0.0)
    hop = 2**level if isinstance(level, int) else jnp.left_shift(1, level)
    back = 128 - hop
    inverse = block_inverse(mid)
    alpha = [-x for x in block_product(low, shifted(inverse, hop))]
    gamma = [-x for x in block_product(up, shifted(inverse, back))]
    write_factor(write_ref, joined(alpha), unit, joined(gamma), hop)
    add_low = block_product(alpha, shifted(up, hop))
    add_up = block_product(gamma, shifted(low, back))
    mid = tuple(m + a + b for m, a, b in zip(mid, add_low, add_up))
    new_low = tuple(block_product(alpha, shifted(low, hop)))
    new_up = tuple(block_product(gamma, shifted(up, back)))
    return new_low, mid, new_up


def reduce_levels(parts, left_ref, factor_ref, first, last):
    def one_level(level, carry):
        carry = reduce_level(level, carry, factor_ref)
        times_factor(left_ref, factor_ref)
        return carry

    return lax.fori_loop(first, last, one_level, parts)


def finish_operator(parts, left_ref, factor_ref, terms_ref, design_ref, high_ref, low_ref):
    inverse = joined(block_inverse(parts[1]))
    write_factor(factor_ref, None, inverse, None, 0)
    times_factor(left_ref, factor_ref)
    x = left_ref[...]
    x1, x2 = split2(x)
    terms_ref[0] = x1
    terms_ref[1] = x2
    terms_ref[2] = (x - x1.astype(f32) - x2.astype(f32)).astype(bf16)

    def one_block(step, carry):
        at = pl.multiple_of(step * 128, 128)
        date = iota((128, DATES), 0) + at
        position = iota((128, DATES), 1)
        order = jnp.where(
            (position % BLOCKS) * 8 + position // BLOCKS == date, 1.0, 0.0
        ).astype(bf16)
        m = jnp.zeros((128, PAIRS), f32)
        for term in (2, 1, 0):
            m = m + dot(dot(order, terms_ref[term]).astype(bf16), design_ref[...])
        high, low = split2(m)
        high_ref[pl.ds(at, 128), :] = high
        low_ref[pl.ds(at, 128), :] = low
        return carry

    lax.fori_loop(0, DATES // 128, one_block, 0)


def own_code_rows(u, numbers_ref, places_ref, own_codes_ref):
    block = iota((GROUPS, TILES), 0)
    code = jnp.where(block < numbers_ref[...], places_ref[...], SLOTS).astype(f32)
    lane = iota((GROUPS, 128), 1)
    group = iota((GROUPS, 128), 0)
    spread = (lane // LOOKS % GROUPS == group) & (lane // 16 == lax.rem(u, 8))
    rows = lax.dot_general(
        code.astype(bf16),
        jnp.where(spread, 1.0, 0.0).astype(bf16),
        (((0,), (0,)), ((), ())),
        preferred_element_type=f32,
    )
    own_codes_ref[...] = rows.reshape(TILES, 1, 128)


def place_group(slot, pix, parity, part, landed_ref, codes_ref, stack_ref, swapped_ref):
    half = iota((128, 128), 1) < 64
    blocks = landed_ref[part * 8 : (part + 1) * 8, parity, pix].reshape(128, 128)
    row = codes_ref[pix, pl.ds(parity * 4 + part, 1), :]
    chooser = jnp.where(slot == row, 1.0, 0.0).astype(bf16)
    turned = pltpu.roll(blocks.astype(f32), 64, 1)
    turned = jnp.where(half, -turned, turned).astype(bf16)
    placed = dot(chooser, jnp.concatenate([blocks, turned], axis=1))
    for q in range(8):
        date = (2 * (8 * part + q) + parity) * 8 + pix
        stack_ref[date] = placed[q * 32 : (q + 1) * 32, :128]
        swapped_ref[date] = placed[q * 32 : (q + 1) * 32, 128:]


def exchange_kernel(
    x_hbm, w_ref, couples_ref, pairs_ref, numbers_ref, places_ref,
    out_ref,
    x_ref, own_codes_ref, c_mid, c_sum, c_all, landed_ref, high_ref, low_ref,
    stack_ref, swapped_ref, phase_ref,
    e_ref, spread_ref, o_ref, z_mid, d_mid, design_ref, left_ref, factor_ref, terms_ref,
    send_z1, recv_z1, send_d1, recv_d1, send_d2, recv_d2, send_z2, recv_z2, local_sem, x_sem,
    send_c1, recv_c1, send_c2, recv_c2,
):
    a = lax.axis_index("date")
    z = lax.axis_index("pix")
    core = lax.rem(a, 2)
    other = 1 - core
    u = lax.div(a, 2)

    def z_of(step):
        return lax.rem(z + step, N_PIX)

    def u_of(step):
        return lax.rem(u + step, HALF_TILES)

    def chunk_of(step):
        return 4 + (1 - 2 * lax.rem(step, 2)) * lax.div(step + 1, 2)

    def load_chunk(step):
        at = lax.rem(lax.div(u, 4) + chunk_of(step), 8)
        rows = pl.ds(pl.multiple_of(at * 1024, 1024), 1024)
        return pltpu.make_async_copy(x_hbm.at[rows], x_ref.at[rows], x_sem.at[step])

    def each(first, last, act):
        def body(step, carry):
            act(step)
            return carry

        lax.fori_loop(first, last, body, 0)

    each(0, 8, lambda s: load_chunk(s).start())

    barrier = pltpu.get_barrier_semaphore()

    def greet(device):
        pl.semaphore_signal(barrier, inc=1, device_id=device, device_id_type=MESH)

    def greet_pix(step, carry):
        greet((a, z_of(step)))
        return carry

    def greet_same(step, carry):
        greet((2 * u_of(step) + core, z))
        return carry

    def greet_other(step, carry):
        greet((2 * u_of(step) + other, z))
        return carry

    lax.fori_loop(1, N_PIX, greet_pix, 0)
    lax.fori_loop(1, HALF_TILES, greet_same, 0)
    lax.fori_loop(0, HALF_TILES, greet_other, 0)

    build_row_matrix(w_ref, e_ref)
    own_code_rows(u, numbers_ref, places_ref, own_codes_ref)

    pl.semaphore_wait(barrier, N_PIX - 1 + HALF_TILES - 1 + HALF_TILES)

    def pix_first(step):
        to = z_of(step)
        return pltpu.make_async_remote_copy(
            src_ref=o_ref.at[:, core, to], dst_ref=z_mid.at[z],
            send_sem=send_z1.at[step], recv_sem=recv_z1.at[step],
            device_id=(a, to), device_id_type=MESH,
        )

    def pix_first_part(step, at):
        to = z_of(step)
        tiles = pl.ds(at * 4, 4)
        return pltpu.make_async_remote_copy(
            src_ref=o_ref.at[tiles, core, to], dst_ref=z_mid.at[z, tiles],
            send_sem=send_z1.at[step], recv_sem=recv_z1.at[step],
            device_id=(a, to), device_id_type=MESH,
        )

    def tile_near(down, across):
        return lax.rem(lax.div(u, 4) + down, 8) * 4 + lax.rem(u + across, 4)

    def date_first(down, across):
        to = tile_near(down, across)
        return pltpu.make_async_remote_copy(
            src_ref=o_ref.at[to, other], dst_ref=d_mid.at[u],
            send_sem=send_d1.at[down * 4 + across], recv_sem=recv_d1.at[down * 4 + across],
            device_id=(2 * to + other, z), device_id_type=MESH,
        )

    def date_second(step):
        to = u_of(step)
        return pltpu.make_async_remote_copy(
            src_ref=z_mid.at[:, to], dst_ref=landed_ref.at[u, core],
            send_sem=send_d2.at[step], recv_sem=recv_d2.at[step],
            device_id=(2 * to + core, z), device_id_type=MESH,
        )

    def pix_second(step):
        to = z_of(step)
        return pltpu.make_async_remote_copy(
            src_ref=d_mid.at[:, to], dst_ref=landed_ref.at[:, other, z],
            send_sem=send_z2.at[step], recv_sem=recv_z2.at[step],
            device_id=(a, to), device_id_type=MESH,
        )

    def arrival_pix_first(step):
        at = lax.rem(z + N_PIX - step, N_PIX)
        return pltpu.make_async_remote_copy(
            src_ref=o_ref.at[:, core, at], dst_ref=z_mid.at[at],
            send_sem=send_z1.at[step], recv_sem=recv_z1.at[step],
            device_id=(a, at), device_id_type=MESH,
        )

    def arrival_date_first(step):
        down = lax.div(step, 4)
        across = lax.rem(step, 4)
        at = tile_near(8 - down, 4 - across)
        return pltpu.make_async_remote_copy(
            src_ref=o_ref.at[at, other], dst_ref=d_mid.at[at],
            send_sem=send_d1.at[step], recv_sem=recv_d1.at[step],
            device_id=(2 * at + other, z), device_id_type=MESH,
        )

    def arrival_date_second(step):
        at = lax.rem(u + HALF_TILES - step, HALF_TILES)
        return pltpu.make_async_remote_copy(
            src_ref=z_mid.at[:, at], dst_ref=landed_ref.at[at, core],
            send_sem=send_d2.at[step], recv_sem=recv_d2.at[step],
            device_id=(2 * at + core, z), device_id_type=MESH,
        )

    def arrival_pix_second(step):
        at = lax.rem(z + N_PIX - step, N_PIX)
        return pltpu.make_async_remote_copy(
            src_ref=d_mid.at[:, at], dst_ref=landed_ref.at[:, other, at],
            send_sem=send_z2.at[step], recv_sem=recv_z2.at[step],
            device_id=(a, at), device_id_type=MESH,
        )

    def code_to_other(step):
        to = 2 * u_of(step) + other
        return pltpu.make_async_remote_copy(
            src_ref=own_codes_ref.at[to], dst_ref=c_mid.at[a],
            send_sem=send_c1.at[step], recv_sem=recv_c1.at[step],
            device_id=(to, z), device_id_type=MESH,
        )

    def code_to_same(step):
        to = 2 * u_of(step) + core
        return pltpu.make_async_remote_copy(
            src_ref=own_codes_ref.at[to], dst_ref=c_mid.at[a],
            send_sem=send_c1.at[HALF_TILES + step], recv_sem=recv_c1.at[HALF_TILES + step],
            device_id=(to, z), device_id_type=MESH,
        )

    def arrival_code_other(step):
        at = 2 * lax.rem(u + HALF_TILES - step, HALF_TILES) + other
        return pltpu.make_async_remote_copy(
            src_ref=own_codes_ref.at[at], dst_ref=c_mid.at[at],
            send_sem=send_c1.at[step], recv_sem=recv_c1.at[step],
            device_id=(at, z), device_id_type=MESH,
        )

    def arrival_code_same(step):
        at = 2 * lax.rem(u + HALF_TILES - step, HALF_TILES) + core
        return pltpu.make_async_remote_copy(
            src_ref=own_codes_ref.at[at], dst_ref=c_mid.at[at],
            send_sem=send_c1.at[HALF_TILES + step], recv_sem=recv_c1.at[HALF_TILES + step],
            device_id=(at, z), device_id_type=MESH,
        )

    def code_second(step):
        to = z_of(step)
        return pltpu.make_async_remote_copy(
            src_ref=c_sum, dst_ref=c_all.at[z],
            send_sem=send_c2.at[step], recv_sem=recv_c2.at[step],
            device_id=(a, to), device_id_type=MESH,
        )

    def arrival_code_second(step):
        at = lax.rem(z + N_PIX - step, N_PIX)
        return pltpu.make_async_remote_copy(
            src_ref=c_sum, dst_ref=c_all.at[at],
            send_sem=send_c2.at[step], recv_sem=recv_c2.at[step],
            device_id=(a, at), device_id_type=MESH,
        )

    pick = row_picker()

    def send_chunk(step):
        down = chunk_of(step)
        at = lax.rem(lax.div(u, 4) + down, 8)
        load_chunk(step).wait()
        resample_chunk(at, pick, x_ref, e_ref, spread_ref, o_ref)
        for across in range(4):
            date_first(down, across).start()
        each(1, N_PIX, lambda s: pix_first_part(s, at).start())

    each(0, 8, send_chunk)
    own_first = pltpu.make_async_copy(o_ref.at[:, core, z], z_mid.at[z], local_sem.at[0])
    own_first.start()
    each(0, HALF_TILES, lambda s: code_to_other(s).start())
    each(1, HALF_TILES, lambda s: code_to_same(s).start())
    c_mid[a] = own_codes_ref[a]

    parts = normal_parts(couples_ref, design_ref)
    parts = reduce_level(0, parts, left_ref)
    parts = reduce_levels(parts, left_ref, factor_ref, 1, EARLY_LEVELS)

    each(0, HALF_TILES, lambda s: arrival_code_other(s).wait_recv())
    each(1, HALF_TILES, lambda s: arrival_code_same(s).wait_recv())
    for e in range(2):
        for p in range(4):
            total = c_mid[16 * p + e]
            for q in range(1, 8):
                total = total + c_mid[16 * p + 2 * q + e]
            c_sum[4 * e + p : 4 * e + p + 1, :] = total
    c_all[z] = c_sum[...]
    each(1, N_PIX, lambda s: code_second(s).start())

    own_first.wait()
    each(1, N_PIX, lambda s: arrival_pix_first(s).wait_recv())
    each(1, HALF_TILES, lambda s: date_second(s).start())
    own_date = pltpu.make_async_copy(
        z_mid.at[:, u], landed_ref.at[u, core], local_sem.at[1]
    )
    own_date.start()
    each(0, HALF_TILES, lambda s: arrival_date_first(s).wait_recv())
    each(1, N_PIX, lambda s: pix_second(s).start())
    own_pix = pltpu.make_async_copy(
        d_mid.at[:, z], landed_ref.at[:, other, z], local_sem.at[2]
    )
    own_pix.start()

    parts = reduce_levels(parts, left_ref, factor_ref, EARLY_LEVELS, 6)
    finish_operator(parts, left_ref, factor_ref, terms_ref, design_ref, high_ref, low_ref)

    each(1, N_PIX, lambda s: arrival_code_second(s).wait_recv())

    row = iota((256, 128), 0)
    column = iota((256, 128), 1)
    fits = (row // 32 == column // 16) & (row // 8 % 4 == column % 4)
    slot = jnp.where(fits, row % 8, -1).astype(f32)

    def place_pix(pix, parity):
        for part in range(4):
            place_group(slot, pix, parity, part, landed_ref, c_all, stack_ref, swapped_ref)

    def land_pix(step):
        arrival_pix_second(step).wait_recv()
        place_pix(lax.rem(z + N_PIX - step, N_PIX), other)

    own_pix.wait()
    place_pix(z, other)
    each(1, N_PIX, land_pix)
    own_date.wait()
    each(1, HALF_TILES, lambda s: arrival_date_second(s).wait_recv())
    each(0, N_PIX, lambda pix: place_pix(pix, core))

    solve_phases(pairs_ref, high_ref, low_ref, out_ref, stack_ref, swapped_ref, phase_ref)

    each(0, HALF_TILES, lambda s: code_to_other(s).wait_send())
    each(1, HALF_TILES, lambda s: code_to_same(s).wait_send())
    each(1, N_PIX, lambda s: code_second(s).wait_send())
    each(1, N_PIX, lambda s: pix_first(s).wait_send())
    each(0, HALF_TILES, lambda s: date_first(lax.div(s, 4), lax.rem(s, 4)).wait_send())
    each(1, HALF_TILES, lambda s: date_second(s).wait_send())
    each(1, N_PIX, lambda s: pix_second(s).wait_send())


def solve_phases(pairs_ref, high_ref, low_ref, out_ref, stack_ref, swapped_ref, phase_ref):
    low_half = iota((8, 128), 1) < 64

    def one_pair(k):
        earlier = stack_ref[pairs_ref[0, k]]
        later = pairs_ref[1, k]
        real = earlier * stack_ref[later]
        imag = earlier * swapped_ref[later]

        def looks(v):
            return (v[0:8] + v[8:16]) + (v[16:24] + v[24:32])

        return looks(real), looks(imag)

    def merge(v, w):
        return jnp.where(low_half, v, w) + pltpu.roll(jnp.where(low_half, w, v), 64, 1)

    def pairs(step, carry):
        found = [
            (one_pair(step * BATCH + q), one_pair(step * BATCH + q + HALF))
            for q in range(BATCH)
        ]
        phases = []
        for (r0, i0), (r1, i1) in found:
            real = merge(r0, r1)
            imag = merge(i0, i1)
            power = jnp.maximum(real * real + imag * imag, float(LOOKS * LOOKS))
            phases.append(imag * lax.rsqrt(power))
        to = pl.ds(pl.multiple_of(step * (8 * BATCH), 8 * BATCH), 8 * BATCH)
        phase_ref[to, :] = jnp.concatenate(phases, axis=0)
        return carry

    lax.fori_loop(0, HALF // BATCH, pairs, 0)

    wide = iota((HALF, 128), 1) < 64
    for part in range(2):
        columns = []
        for p in (2 * part, 2 * part + 1):
            a0 = phase_ref[pl.ds(2 * p, HALF, stride=8), :]
            a1 = phase_ref[pl.ds(2 * p + 1, HALF, stride=8), :]
            columns.append(
                jnp.concatenate(
                    [
                        jnp.where(wide, a0, pltpu.roll(a1, 64, 1)),
                        jnp.where(wide, pltpu.roll(a0, 64, 1), a1),
                    ],
                    axis=0,
                )
            )
        high, low = split2(jnp.concatenate(columns, axis=1))
        out_ref[:, part * 256 : (part + 1) * 256] = dot(high_ref[...], high) + (
            dot(high_ref[...], low) + dot(low_ref[...], high)
        )


def exchange(x, w, couples, numbers, places):
    vmem = pl.BlockSpec(memory_space=pltpu.VMEM)
    smem = pl.BlockSpec(memory_space=pltpu.SMEM)
    dma = pltpu.SemaphoreType.DMA
    return pl.pallas_call(
        exchange_kernel,
        out_shape=jax.ShapeDtypeStruct((DATES, 512), f32),
        in_specs=[pl.BlockSpec(memory_space=pl.ANY), smem, vmem, smem, vmem, vmem],
        out_specs=vmem,
        scratch_shapes=[
            pltpu.VMEM((TILES * 128, 128), bf16),
            pltpu.VMEM((TILES, 1, 128), f32),
            pltpu.VMEM((TILES, 1, 128), f32),
            pltpu.VMEM((8, 128), f32),
            pltpu.VMEM((N_PIX, 8, 128), f32),
            pltpu.VMEM((HALF_TILES, 2, N_PIX, 16, 128), bf16),
            pltpu.VMEM((DATES, PAIRS), bf16),
            pltpu.VMEM((DATES, PAIRS), bf16),
            pltpu.VMEM((DATES, 32, 128), f32),
            pltpu.VMEM((DATES, 32, 128), f32),
            pltpu.VMEM((HALF * 8, 128), f32),
            pltpu.VMEM((512, 512), bf16),
            pltpu.VMEM((CHUNK * 128, 128), f32),
            pltpu.VMEM((HALF_TILES, 2, N_PIX, 16, 128), bf16),
            pltpu.VMEM((N_PIX, HALF_TILES, 16, 128), bf16),
            pltpu.VMEM((HALF_TILES, N_PIX, 16, 128), bf16),
            pltpu.VMEM((DATES, PAIRS), bf16),
            pltpu.VMEM((DATES, DATES), f32),
            pltpu.VMEM((DATES, DATES), f32),
            pltpu.VMEM((3, DATES, DATES), bf16),
            dma((N_PIX,)), dma((N_PIX,)),
            dma((HALF_TILES,)), dma((HALF_TILES,)),
            dma((HALF_TILES,)), dma((HALF_TILES,)),
            dma((N_PIX,)), dma((N_PIX,)),
            dma((3,)), dma((8,)),
            dma((2 * HALF_TILES,)), dma((2 * HALF_TILES,)),
            dma((N_PIX,)), dma((N_PIX,)),
        ],
        compiler_params=pltpu.CompilerParams(
            collective_id=0, has_side_effects=True, vmem_limit_bytes=VMEM_BYTES
        ),
        name="exchange",
    )(x, w, couples, couples, numbers, places)


def local(scene_groups, weights, numbers, places, couples):
    return exchange(
        scene_groups.reshape(TILES * 128, 128), weights, couples.T, numbers, places[0].T
    )


def solution(mesh):
    in_specs = (
        P(("date", "pix"), None, None, None, None, None),
        P(("date", "pix"), None),
        P(("date", "pix"), None),
        P(("date", "pix"), None, None),
        P(),
    )
    out_specs = P(None, ("date", "pix"))
    return jax.shard_map(local, mesh=mesh, in_specs=in_specs, out_specs=out_specs, check_vma=False)
```

```python
import jax
import jax.numpy as jnp
from jax import lax
from jax.experimental import pallas as pl
from jax.experimental.pallas import tpu as pltpu
from jax.sharding import PartitionSpec as P

ALONG_TRACK_LINES = 128
LOOKS = 4
TAPS = 8
GROUPS = 4
SLOTS = 8
PAIRS = 1200
DATES = 512
HALF = PAIRS // 2
BLOCKS = 64
TILES = 64
HALF_TILES = 32
N_PIX = 8
CHUNK = 8
BATCH = 40
EARLY_LEVELS = 4
VMEM_BYTES = 56 * 1024 * 1024
MESH = pl.DeviceIdType.MESH
f32 = jnp.float32
bf16 = jnp.bfloat16
HIGHEST = lax.Precision.HIGHEST


def iota(shape, dim):
    return lax.broadcasted_iota(jnp.int32, shape, dim)


def dot(a, b):
    return jnp.dot(a, b, preferred_element_type=f32)


def split2(x):
    high = x.astype(bf16)
    low = (x - high.astype(f32)).astype(bf16)
    return high, low


def build_row_matrix(w_ref, e_ref):
    lane = iota((128, 128), 1)
    lag = iota((128, 128), 0) - 4 * (lane % 32) + TAPS // 2
    for j in range(LOOKS):
        taps = jnp.zeros((128, 128), f32)
        for tap in range(TAPS):
            taps = jnp.where(lag - j == tap, w_ref[0, tap], taps)
        for g in range(4):
            e_ref[g * 128 : (g + 1) * 128, j * 128 : (j + 1) * 128] = jnp.where(
                lane // 32 == g, taps, 0.0
            ).astype(bf16)


def resample_chunk(at, to, pick, x_ref, e_ref, spread_ref, o_ref):
    parts = []
    for k in range(CHUNK):
        rows = pl.ds(pl.multiple_of((at * CHUNK + k) * 128, 128), 128)
        g = dot(pick, x_ref[rows, :]).astype(bf16)
        parts.append(jnp.concatenate([g[32 * q : 32 * (q + 1)] for q in range(4)], axis=1))
    y = dot(jnp.concatenate(parts, axis=0), e_ref[...])
    for j in range(LOOKS):
        spread_ref[pl.ds(j, CHUNK * 32, stride=LOOKS), :] = y[:, j * 128 : (j + 1) * 128]
    for k in range(CHUNK // 2):
        o_ref[to * (CHUNK // 2) + k] = (
            spread_ref[k * 256 : (k + 1) * 256, :].astype(bf16).reshape(2, 8, 16, 128)
        )


def row_picker():
    row = iota((128, 128), 0)
    column = iota((128, 128), 1)
    source = (row % 4) * 32 + (row // 64) * 16 + (row // 4 % 8) * 2 + row // 32 % 2
    return jnp.where(source == column, 1.0, 0.0).astype(bf16)


def block_inverse(rows):
    sub = iota((8, 128), 0)
    rows = list(rows)
    for k in range(8):
        inverse = 1.0 / rows[k][k : k + 1, :]
        pivot = jnp.where(sub == k, inverse, rows[k] * inverse)
        for r in range(8):
            if r != k:
                rows[r] = jnp.where(sub == k, 0.0, rows[r]) - rows[r][k : k + 1, :] * pivot
        rows[k] = pivot
    return rows


def block_product(a, b):
    out = []
    for r in range(8):
        total = a[r][0:1, :] * b[0]
        for k in range(1, 8):
            total = total + a[r][k : k + 1, :] * b[k]
        out.append(total)
    return out


def shifted(rows, amount):
    return [pltpu.roll(x, amount, 1) for x in rows]


def joined(rows):
    lane = iota((8, 128), 1)
    return jnp.concatenate(
        [
            jnp.where(lane < 64, rows[2 * q], pltpu.roll(rows[2 * q + 1], 64, 1))
            for q in range(4)
        ],
        axis=1,
    )


def normal_parts(couples_ref, design_ref):
    position = iota((DATES, PAIRS), 0)
    date = (position % BLOCKS) * 8 + position // BLOCKS
    later = jnp.where(date == couples_ref[1:2, :], 1.0, 0.0)
    earlier = jnp.where(date == couples_ref[0:1, :], 1.0, 0.0)
    design_ref[...] = (later - earlier).astype(bf16)
    lane = iota((BLOCKS, 512), 1)
    offset = iota((BLOCKS, 512), 0) - lane % BLOCKS
    parts = {-1: [], 0: [], 1: []}
    for c in range(8):
        rows = lax.dot_general(
            design_ref[c * 64 : (c + 1) * 64, :],
            design_ref[...],
            (((1,), (1,)), ((), ())),
            preferred_element_type=f32,
        )
        rows = rows + jnp.where((offset == 0) & (lane // BLOCKS == c), 1.0, 0.0)
        for at in parts:
            parts[at].append(
                jnp.sum(jnp.where(offset == at, rows, 0.0), axis=0, keepdims=True)
            )
    small = iota((8, 128), 1)
    sub = iota((8, 128), 0)
    out = []
    for at in (-1, 0, 1):
        whole = jnp.concatenate(parts[at], axis=0)
        rows = []
        for r in range(8):
            x = whole[:, (r // 2) * 128 : (r // 2 + 1) * 128]
            if r % 2:
                x = pltpu.roll(x, 64, 1)
            pad = jnp.where(sub == r, 1.0, 0.0) if at == 0 else jnp.zeros((8, 128), f32)
            rows.append(jnp.where(small < 64, x, pad))
        out.append(tuple(rows))
    return tuple(out)


def write_factor(factor_ref, before, at, after, hop):
    lane = iota((BLOCKS, 512), 1)
    offset = iota((BLOCKS, 512), 0) - lane % BLOCKS
    for c in range(8):
        x = jnp.where(offset == 0, at[c : c + 1, :], 0.0)
        if before is not None:
            x = jnp.where(offset == -hop, before[c : c + 1, :], x)
            x = jnp.where(offset == hop, after[c : c + 1, :], x)
        factor_ref[c * 64 : (c + 1) * 64, :] = x


def times_factor(left_ref, factor_ref):
    def one_block(step, carry):
        at = pl.multiple_of(step * 128, 128)
        rows = pl.ds(at, 128)
        left_ref[rows, :] = jnp.dot(
            left_ref[rows, :], factor_ref[...], preferred_element_type=f32, precision=HIGHEST
        )
        return carry

    lax.fori_loop(0, 4, one_block, 0)


def reduce_level(level, parts, write_ref):
    low, mid, up = parts
    unit = jnp.where(iota((8, 512), 0) == iota((8, 512), 1) // BLOCKS, 1.0, 0.0)
    hop = 2**level if isinstance(level, int) else jnp.left_shift(1, level)
    back = 128 - hop
    inverse = block_inverse(mid)
    alpha = [-x for x in block_product(low, shifted(inverse, hop))]
    gamma = [-x for x in block_product(up, shifted(inverse, back))]
    write_factor(write_ref, joined(alpha), unit, joined(gamma), hop)
    add_low = block_product(alpha, shifted(up, hop))
    add_up = block_product(gamma, shifted(low, back))
    mid = tuple(m + a + b for m, a, b in zip(mid, add_low, add_up))
    new_low = tuple(block_product(alpha, shifted(low, hop)))
    new_up = tuple(block_product(gamma, shifted(up, back)))
    return new_low, mid, new_up


def reduce_levels(parts, left_ref, factor_ref, first, last):
    def one_level(level, carry):
        carry = reduce_level(level, carry, factor_ref)
        times_factor(left_ref, factor_ref)
        return carry

    return lax.fori_loop(first, last, one_level, parts)


def finish_operator(parts, left_ref, factor_ref, terms_ref, design_ref, high_ref, low_ref):
    inverse = joined(block_inverse(parts[1]))
    write_factor(factor_ref, None, inverse, None, 0)
    times_factor(left_ref, factor_ref)
    x = left_ref[...]
    x1, x2 = split2(x)
    terms_ref[0] = x1
    terms_ref[1] = x2
    terms_ref[2] = (x - x1.astype(f32) - x2.astype(f32)).astype(bf16)

    def one_block(step, carry):
        at = pl.multiple_of(step * 128, 128)
        date = iota((128, DATES), 0) + at
        position = iota((128, DATES), 1)
        order = jnp.where(
            (position % BLOCKS) * 8 + position // BLOCKS == date, 1.0, 0.0
        ).astype(bf16)
        m = jnp.zeros((128, PAIRS), f32)
        for term in (2, 1, 0):
            m = m + dot(dot(order, terms_ref[term]).astype(bf16), design_ref[...])
        high, low = split2(m)
        high_ref[pl.ds(at, 128), :] = high
        low_ref[pl.ds(at, 128), :] = low
        return carry

    lax.fori_loop(0, DATES // 128, one_block, 0)


def own_code_rows(u, numbers_ref, places_ref, own_codes_ref):
    block = iota((GROUPS, TILES), 0)
    code = jnp.where(block < numbers_ref[...], places_ref[...], SLOTS).astype(f32)
    lane = iota((GROUPS, 128), 1)
    group = iota((GROUPS, 128), 0)
    spread = (lane // LOOKS % GROUPS == group) & (lane // 16 == lax.rem(u, 8))
    rows = lax.dot_general(
        code.astype(bf16),
        jnp.where(spread, 1.0, 0.0).astype(bf16),
        (((0,), (0,)), ((), ())),
        preferred_element_type=f32,
    )
    own_codes_ref[...] = rows.reshape(TILES, 1, 128)


def place_group(slot, pix, parity, part, landed_ref, codes_ref, stack_ref, swapped_ref):
    half = iota((128, 128), 1) < 64
    blocks = landed_ref[pl.ds(part * 8, 8), parity, pix].reshape(128, 128)
    row = codes_ref[pix, pl.ds(parity * 4 + part, 1), :]
    chooser = jnp.where(slot == row, 1.0, 0.0).astype(bf16)
    turned = pltpu.roll(blocks.astype(f32), 64, 1)
    turned = jnp.where(half, -turned, turned).astype(bf16)
    placed = dot(chooser, jnp.concatenate([blocks, turned], axis=1))
    for q in range(8):
        date = (2 * (8 * part + q) + parity) * 8 + pix
        stack_ref[date] = placed[q * 32 : (q + 1) * 32, :128]
        swapped_ref[date] = placed[q * 32 : (q + 1) * 32, 128:]


def exchange_kernel(
    x_hbm, w_ref, couples_ref, pairs_ref, numbers_ref, places_ref,
    out_ref,
    x_ref, own_codes_ref, c_mid, c_sum, c_all, landed_ref, high_ref, low_ref,
    stack_ref, swapped_ref, phase_ref,
    e_ref, spread_ref, o_ref, z_mid, d_mid, design_ref, left_ref, factor_ref, terms_ref,
    send_z1, recv_z1, send_d1, recv_d1, send_d2, recv_d2, send_z2, recv_z2, local_sem, x_sem,
    send_c1, recv_c1, send_c2, recv_c2,
):
    a = lax.axis_index("date")
    z = lax.axis_index("pix")
    core = lax.rem(a, 2)
    other = 1 - core
    u = lax.div(a, 2)

    def z_of(step):
        return lax.rem(z + step, N_PIX)

    def u_of(step):
        return lax.rem(u + step, HALF_TILES)

    def chunk_of(step):
        return 4 + (1 - 2 * lax.rem(step, 2)) * lax.div(step + 1, 2)

    def load_chunk(step):
        at = lax.rem(lax.div(u, 4) + chunk_of(step), 8)
        rows = pl.ds(pl.multiple_of(at * 1024, 1024), 1024)
        return pltpu.make_async_copy(x_hbm.at[rows], x_ref.at[rows], x_sem.at[step])

    def each(first, last, act):
        def body(step, carry):
            act(step)
            return carry

        lax.fori_loop(first, last, body, 0)

    each(0, 8, lambda s: load_chunk(s).start())

    barrier = pltpu.get_barrier_semaphore()

    def greet(device):
        pl.semaphore_signal(barrier, inc=1, device_id=device, device_id_type=MESH)

    def greet_pix(step, carry):
        greet((a, z_of(step)))
        return carry

    def greet_same(step, carry):
        greet((2 * u_of(step) + core, z))
        return carry

    def greet_other(step, carry):
        greet((2 * u_of(step) + other, z))
        return carry

    lax.fori_loop(1, N_PIX, greet_pix, 0)
    lax.fori_loop(1, HALF_TILES, greet_same, 0)
    lax.fori_loop(0, HALF_TILES, greet_other, 0)

    build_row_matrix(w_ref, e_ref)
    own_code_rows(u, numbers_ref, places_ref, own_codes_ref)

    pl.semaphore_wait(barrier, N_PIX - 1 + HALF_TILES - 1 + HALF_TILES)

    def remote(src, dst, send, recv, device):
        return pltpu.make_async_remote_copy(
            src_ref=src, dst_ref=dst, send_sem=send, recv_sem=recv,
            device_id=device, device_id_type=MESH,
        )

    row = lax.div(u, 4)

    def pix_first(step, first):
        to = z_of(step)
        tiles = slice(first, first + 16)
        return remote(
            o_ref.at[tiles, core, to], z_mid.at[z, tiles],
            send_z1.at[0], recv_z1.at[0], (a, to),
        )

    def date_first(place, across):
        x = lax.rem(u + across, 4)
        to = lax.rem(row + place + 2, 8) * 4 + x
        return remote(
            o_ref.at[place * 4 + x, other], d_mid.at[u],
            send_d1.at[0], recv_d1.at[0], (2 * to + other, z),
        )

    def date_second(step):
        place = lax.div(step, 4)
        x = lax.rem(u + step, 4)
        to = lax.rem(row + place + 2, 8) * 4 + x
        return remote(
            z_mid.at[:, place * 4 + x], landed_ref.at[u, core],
            send_d2.at[0], recv_d2.at[lax.div(u, 8)], (2 * to + core, z),
        )

    def pix_second(step):
        to = z_of(step)
        return remote(
            d_mid.at[:, to], landed_ref.at[:, other, z],
            send_z2.at[0], recv_z2.at[step], (a, to),
        )

    def code_first(step, parity):
        to = 2 * u_of(step) + parity
        return remote(
            own_codes_ref.at[to], c_mid.at[a], send_c1.at[0], recv_c1.at[0], (to, z)
        )

    def code_second(step):
        return remote(
            c_sum, c_all.at[z], send_c2.at[0], recv_c2.at[step], (a, z_of(step))
        )

    def arrived(ref, sem):
        remote(ref, ref, sem, sem, (a, z_of(1))).wait_recv()

    def departed(ref, sem):
        remote(ref, ref, sem, sem, (a, z_of(1))).wait_send()

    pick = row_picker()

    def send_chunk(step):
        down = chunk_of(step)
        place = lax.rem(down + 6, 8)
        load_chunk(step).wait()
        resample_chunk(
            lax.rem(row + down, 8), place, pick, x_ref, e_ref, spread_ref, o_ref
        )
        for across in range(4):
            date_first(place, across).start()

    each(0, 4, send_chunk)
    each(1, N_PIX, lambda s: pix_first(s, 0).start())
    each(4, 8, send_chunk)
    each(1, N_PIX, lambda s: pix_first(s, 16).start())
    pltpu.make_async_copy(o_ref.at[:, core, z], z_mid.at[z], recv_z1.at[0]).start()
    each(0, HALF_TILES, lambda s: code_first(s, other).start())
    each(1, HALF_TILES, lambda s: code_first(s, core).start())
    pltpu.make_async_copy(own_codes_ref.at[a], c_mid.at[a], recv_c1.at[0]).start()

    parts = normal_parts(couples_ref, design_ref)
    parts = reduce_level(0, parts, left_ref)
    parts = reduce_levels(parts, left_ref, factor_ref, 1, EARLY_LEVELS)

    arrived(c_mid, recv_c1.at[0])
    for e in range(2):
        for p in range(4):
            total = c_mid[16 * p + e]
            for q in range(1, 8):
                total = total + c_mid[16 * p + 2 * q + e]
            c_sum[4 * e + p : 4 * e + p + 1, :] = total
    c_all[z] = c_sum[...]
    each(1, N_PIX, lambda s: code_second(s).start())

    arrived(z_mid, recv_z1.at[0])
    each(0, 24, lambda s: date_second(s).start())
    each(25, 32, lambda s: date_second(s).start())
    pltpu.make_async_copy(
        z_mid.at[:, 24 + lax.rem(u, 4)], landed_ref.at[u, core], recv_d2.at[lax.div(u, 8)]
    ).start()
    arrived(d_mid, recv_d1.at[0])
    each(1, N_PIX, lambda s: pix_second(s).start())
    own_pix = pltpu.make_async_copy(
        d_mid.at[:, z], landed_ref.at[:, other, z], local_sem.at[0]
    )
    own_pix.start()

    parts = reduce_levels(parts, left_ref, factor_ref, EARLY_LEVELS, 6)
    finish_operator(parts, left_ref, factor_ref, terms_ref, design_ref, high_ref, low_ref)

    each(1, N_PIX, lambda s: arrived(c_sum, recv_c2.at[s]))

    line = iota((256, 128), 0)
    column = iota((256, 128), 1)
    fits = (line // 32 == column // 16) & (line // 8 % 4 == column % 4)
    slot = jnp.where(fits, line % 8, -1).astype(f32)

    def place(pix, parity, part):
        place_group(slot, pix, parity, part, landed_ref, c_all, stack_ref, swapped_ref)

    def land_pix(step):
        at = lax.rem(z + N_PIX - step, N_PIX)
        arrived(landed_ref.at[:, other, at], recv_z2.at[step])
        for part in range(4):
            place(at, other, part)

    def land_dates(step):
        part = lax.rem(lax.div(u, 8) + 2 + step, 4)
        arrived(landed_ref.at[pl.ds(part * 8, 8), core], recv_d2.at[part])
        for pix in range(N_PIX):
            place(pix, core, part)

    own_pix.wait()
    for part in range(4):
        place(z, other, part)
    each(1, N_PIX, land_pix)
    each(0, 4, land_dates)

    solve_phases(pairs_ref, high_ref, low_ref, out_ref, stack_ref, swapped_ref, phase_ref)

    departed(own_codes_ref.at[0 : TILES - 1], send_c1.at[0])
    departed(c_all.at[0 : N_PIX - 1], send_c2.at[0])
    departed(o_ref.at[:, 0, 0 : N_PIX - 1], send_z1.at[0])
    departed(o_ref.at[:, 0], send_d1.at[0])
    departed(z_mid.at[:, 0 : HALF_TILES - 1], send_d2.at[0])
    departed(d_mid.at[:, 0 : N_PIX - 1], send_z2.at[0])


def solve_phases(pairs_ref, high_ref, low_ref, out_ref, stack_ref, swapped_ref, phase_ref):
    low_half = iota((8, 128), 1) < 64

    def one_pair(k):
        earlier = stack_ref[pairs_ref[0, k]]
        later = pairs_ref[1, k]
        real = earlier * stack_ref[later]
        imag = earlier * swapped_ref[later]

        def looks(v):
            return (v[0:8] + v[8:16]) + (v[16:24] + v[24:32])

        return looks(real), looks(imag)

    def merge(v, w):
        return jnp.where(low_half, v, w) + pltpu.roll(jnp.where(low_half, w, v), 64, 1)

    def pairs(step, carry):
        found = [
            (one_pair(step * BATCH + q), one_pair(step * BATCH + q + HALF))
            for q in range(BATCH)
        ]
        phases = []
        for (r0, i0), (r1, i1) in found:
            real = merge(r0, r1)
            imag = merge(i0, i1)
            power = jnp.maximum(real * real + imag * imag, float(LOOKS * LOOKS))
            phases.append(imag * lax.rsqrt(power))
        to = pl.ds(pl.multiple_of(step * (8 * BATCH), 8 * BATCH), 8 * BATCH)
        phase_ref[to, :] = jnp.concatenate(phases, axis=0)
        return carry

    lax.fori_loop(0, HALF // BATCH, pairs, 0)

    wide = iota((HALF, 128), 1) < 64
    for part in range(2):
        columns = []
        for p in (2 * part, 2 * part + 1):
            a0 = phase_ref[pl.ds(2 * p, HALF, stride=8), :]
            a1 = phase_ref[pl.ds(2 * p + 1, HALF, stride=8), :]
            columns.append(
                jnp.concatenate(
                    [
                        jnp.where(wide, a0, pltpu.roll(a1, 64, 1)),
                        jnp.where(wide, pltpu.roll(a0, 64, 1), a1),
                    ],
                    axis=0,
                )
            )
        high, low = split2(jnp.concatenate(columns, axis=1))
        out_ref[:, part * 256 : (part + 1) * 256] = dot(high_ref[...], high) + (
            dot(high_ref[...], low) + dot(low_ref[...], high)
        )


def exchange(x, w, couples, numbers, places):
    vmem = pl.BlockSpec(memory_space=pltpu.VMEM)
    smem = pl.BlockSpec(memory_space=pltpu.SMEM)
    dma = pltpu.SemaphoreType.DMA
    return pl.pallas_call(
        exchange_kernel,
        out_shape=jax.ShapeDtypeStruct((DATES, 512), f32),
        in_specs=[pl.BlockSpec(memory_space=pl.ANY), smem, vmem, smem, vmem, vmem],
        out_specs=vmem,
        scratch_shapes=[
            pltpu.VMEM((TILES * 128, 128), bf16),
            pltpu.VMEM((TILES, 1, 128), f32),
            pltpu.VMEM((TILES, 1, 128), f32),
            pltpu.VMEM((8, 128), f32),
            pltpu.VMEM((N_PIX, 8, 128), f32),
            pltpu.VMEM((HALF_TILES, 2, N_PIX, 16, 128), bf16),
            pltpu.VMEM((DATES, PAIRS), bf16),
            pltpu.VMEM((DATES, PAIRS), bf16),
            pltpu.VMEM((DATES, 32, 128), f32),
            pltpu.VMEM((DATES, 32, 128), f32),
            pltpu.VMEM((HALF * 8, 128), f32),
            pltpu.VMEM((512, 512), bf16),
            pltpu.VMEM((CHUNK * 128, 128), f32),
            pltpu.VMEM((HALF_TILES, 2, N_PIX, 16, 128), bf16),
            pltpu.VMEM((N_PIX, HALF_TILES, 16, 128), bf16),
            pltpu.VMEM((HALF_TILES, N_PIX, 16, 128), bf16),
            pltpu.VMEM((DATES, PAIRS), bf16),
            pltpu.VMEM((DATES, DATES), f32),
            pltpu.VMEM((DATES, DATES), f32),
            pltpu.VMEM((3, DATES, DATES), bf16),
            dma((1,)), dma((1,)),
            dma((1,)), dma((1,)),
            dma((1,)), dma((4,)),
            dma((1,)), dma((N_PIX,)),
            dma((1,)), dma((8,)),
            dma((1,)), dma((1,)),
            dma((1,)), dma((N_PIX,)),
        ],
        compiler_params=pltpu.CompilerParams(
            collective_id=0, has_side_effects=True, vmem_limit_bytes=VMEM_BYTES
        ),
        name="exchange",
    )(x, w, couples, couples, numbers, places)


def local(scene_groups, weights, numbers, places, couples):
    return exchange(
        scene_groups.reshape(TILES * 128, 128), weights, couples.T, numbers, places[0].T
    )


def solution(mesh):
    in_specs = (
        P(("date", "pix"), None, None, None, None, None),
        P(("date", "pix"), None),
        P(("date", "pix"), None),
        P(("date", "pix"), None, None),
        P(),
    )
    out_specs = P(None, ("date", "pix"))
    return jax.shard_map(local, mesh=mesh, in_specs=in_specs, out_specs=out_specs, check_vma=False)
```

```python
import jax
import jax.numpy as jnp
from jax import lax
from jax.experimental import pallas as pl
from jax.experimental.pallas import tpu as pltpu
from jax.sharding import PartitionSpec as P

ALONG_TRACK_LINES = 128
LOOKS = 4
TAPS = 8
GROUPS = 4
SLOTS = 8
PAIRS = 1200
DATES = 512
HALF = PAIRS // 2
BLOCKS = 64
TILES = 64
HALF_TILES = 32
N_PIX = 8
CHUNK = 8
BATCH = 40
EARLY_LEVELS = 4
VMEM_BYTES = 56 * 1024 * 1024
MESH = pl.DeviceIdType.MESH
f32 = jnp.float32
bf16 = jnp.bfloat16
HIGHEST = lax.Precision.HIGHEST


def iota(shape, dim):
    return lax.broadcasted_iota(jnp.int32, shape, dim)


def dot(a, b):
    return jnp.dot(a, b, preferred_element_type=f32)


def split2(x):
    high = x.astype(bf16)
    low = (x - high.astype(f32)).astype(bf16)
    return high, low


def build_row_matrix(w_ref, e_ref):
    lane = iota((128, 128), 1)
    lag = iota((128, 128), 0) - 4 * (lane % 32) + TAPS // 2
    for j in range(LOOKS):
        taps = jnp.zeros((128, 128), f32)
        for tap in range(TAPS):
            taps = jnp.where(lag - j == tap, w_ref[0, tap], taps)
        for g in range(4):
            e_ref[g * 128 : (g + 1) * 128, j * 128 : (j + 1) * 128] = jnp.where(
                lane // 32 == g, taps, 0.0
            ).astype(bf16)


def resample_chunk(at, to, pick, x_ref, e_ref, spread_ref, o_ref):
    parts = []
    for k in range(CHUNK):
        rows = pl.ds(pl.multiple_of((at * CHUNK + k) * 128, 128), 128)
        g = dot(pick, x_ref[rows, :]).astype(bf16)
        parts.append(jnp.concatenate([g[32 * q : 32 * (q + 1)] for q in range(4)], axis=1))
    y = dot(jnp.concatenate(parts, axis=0), e_ref[...])
    for j in range(LOOKS):
        spread_ref[pl.ds(j, CHUNK * 32, stride=LOOKS), :] = y[:, j * 128 : (j + 1) * 128]
    for k in range(CHUNK // 2):
        o_ref[to * (CHUNK // 2) + k] = (
            spread_ref[k * 256 : (k + 1) * 256, :].astype(bf16).reshape(2, 8, 16, 128)
        )


def row_picker():
    row = iota((128, 128), 0)
    column = iota((128, 128), 1)
    source = (row % 4) * 32 + (row // 64) * 16 + (row // 4 % 8) * 2 + row // 32 % 2
    return jnp.where(source == column, 1.0, 0.0).astype(bf16)


def block_inverse(rows):
    sub = iota((8, 128), 0)
    rows = list(rows)
    for k in range(8):
        inverse = 1.0 / rows[k][k : k + 1, :]
        pivot = jnp.where(sub == k, inverse, rows[k] * inverse)
        for r in range(8):
            if r != k:
                rows[r] = jnp.where(sub == k, 0.0, rows[r]) - rows[r][k : k + 1, :] * pivot
        rows[k] = pivot
    return rows


def block_product(a, b):
    out = []
    for r in range(8):
        total = a[r][0:1, :] * b[0]
        for k in range(1, 8):
            total = total + a[r][k : k + 1, :] * b[k]
        out.append(total)
    return out


def shifted(rows, amount):
    return [pltpu.roll(x, amount, 1) for x in rows]


def joined(rows):
    lane = iota((8, 128), 1)
    return jnp.concatenate(
        [
            jnp.where(lane < 64, rows[2 * q], pltpu.roll(rows[2 * q + 1], 64, 1))
            for q in range(4)
        ],
        axis=1,
    )


def normal_parts(couples_ref, design_ref):
    position = iota((DATES, PAIRS), 0)
    date = (position % BLOCKS) * 8 + position // BLOCKS
    later = jnp.where(date == couples_ref[1:2, :], 1.0, 0.0)
    earlier = jnp.where(date == couples_ref[0:1, :], 1.0, 0.0)
    design_ref[...] = (later - earlier).astype(bf16)
    lane = iota((BLOCKS, 512), 1)
    offset = iota((BLOCKS, 512), 0) - lane % BLOCKS
    parts = {-1: [], 0: [], 1: []}
    for c in range(8):
        rows = lax.dot_general(
            design_ref[c * 64 : (c + 1) * 64, :],
            design_ref[...],
            (((1,), (1,)), ((), ())),
            preferred_element_type=f32,
        )
        rows = rows + jnp.where((offset == 0) & (lane // BLOCKS == c), 1.0, 0.0)
        for at in parts:
            parts[at].append(
                jnp.sum(jnp.where(offset == at, rows, 0.0), axis=0, keepdims=True)
            )
    small = iota((8, 128), 1)
    sub = iota((8, 128), 0)
    out = []
    for at in (-1, 0, 1):
        whole = jnp.concatenate(parts[at], axis=0)
        rows = []
        for r in range(8):
            x = whole[:, (r // 2) * 128 : (r // 2 + 1) * 128]
            if r % 2:
                x = pltpu.roll(x, 64, 1)
            pad = jnp.where(sub == r, 1.0, 0.0) if at == 0 else jnp.zeros((8, 128), f32)
            rows.append(jnp.where(small < 64, x, pad))
        out.append(tuple(rows))
    return tuple(out)


def write_factor(factor_ref, before, at, after, hop):
    lane = iota((BLOCKS, 512), 1)
    offset = iota((BLOCKS, 512), 0) - lane % BLOCKS
    for c in range(8):
        x = jnp.where(offset == 0, at[c : c + 1, :], 0.0)
        if before is not None:
            x = jnp.where(offset == -hop, before[c : c + 1, :], x)
            x = jnp.where(offset == hop, after[c : c + 1, :], x)
        factor_ref[c * 64 : (c + 1) * 64, :] = x


def times_factor(left_ref, factor_ref):
    def one_block(step, carry):
        at = pl.multiple_of(step * 128, 128)
        rows = pl.ds(at, 128)
        left_ref[rows, :] = jnp.dot(
            left_ref[rows, :], factor_ref[...], preferred_element_type=f32, precision=HIGHEST
        )
        return carry

    lax.fori_loop(0, 4, one_block, 0)


def reduce_level(level, parts, write_ref):
    low, mid, up = parts
    unit = jnp.where(iota((8, 512), 0) == iota((8, 512), 1) // BLOCKS, 1.0, 0.0)
    hop = 2**level if isinstance(level, int) else jnp.left_shift(1, level)
    back = 128 - hop
    inverse = block_inverse(mid)
    alpha = [-x for x in block_product(low, shifted(inverse, hop))]
    gamma = [-x for x in block_product(up, shifted(inverse, back))]
    write_factor(write_ref, joined(alpha), unit, joined(gamma), hop)
    add_low = block_product(alpha, shifted(up, hop))
    add_up = block_product(gamma, shifted(low, back))
    mid = tuple(m + a + b for m, a, b in zip(mid, add_low, add_up))
    new_low = tuple(block_product(alpha, shifted(low, hop)))
    new_up = tuple(block_product(gamma, shifted(up, back)))
    return new_low, mid, new_up


def reduce_levels(parts, left_ref, factor_ref, first, last):
    def one_level(level, carry):
        carry = reduce_level(level, carry, factor_ref)
        times_factor(left_ref, factor_ref)
        return carry

    return lax.fori_loop(first, last, one_level, parts)


def finish_operator(parts, left_ref, factor_ref, terms_ref, design_ref, high_ref, low_ref):
    inverse = joined(block_inverse(parts[1]))
    write_factor(factor_ref, None, inverse, None, 0)
    times_factor(left_ref, factor_ref)
    x = left_ref[...]
    x1, x2 = split2(x)
    terms_ref[0] = x1
    terms_ref[1] = x2
    terms_ref[2] = (x - x1.astype(f32) - x2.astype(f32)).astype(bf16)

    def one_block(step, carry):
        at = pl.multiple_of(step * 128, 128)
        date = iota((128, DATES), 0) + at
        position = iota((128, DATES), 1)
        order = jnp.where(
            (position % BLOCKS) * 8 + position // BLOCKS == date, 1.0, 0.0
        ).astype(bf16)
        m = jnp.zeros((128, PAIRS), f32)
        for term in (2, 1, 0):
            m = m + dot(dot(order, terms_ref[term]).astype(bf16), design_ref[...])
        high, low = split2(m)
        high_ref[pl.ds(at, 128), :] = high
        low_ref[pl.ds(at, 128), :] = low
        return carry

    lax.fori_loop(0, DATES // 128, one_block, 0)


def own_code_rows(u, numbers_ref, places_ref, own_codes_ref):
    block = iota((GROUPS, TILES), 0)
    code = jnp.where(block < numbers_ref[...], places_ref[...], SLOTS).astype(f32)
    lane = iota((GROUPS, 128), 1)
    group = iota((GROUPS, 128), 0)
    spread = (lane // LOOKS % GROUPS == group) & (lane // 16 == lax.rem(u, 8))
    rows = lax.dot_general(
        code.astype(bf16),
        jnp.where(spread, 1.0, 0.0).astype(bf16),
        (((0,), (0,)), ((), ())),
        preferred_element_type=f32,
    )
    own_codes_ref[...] = rows.reshape(TILES, 1, 128)


def place_group(slot, pix, parity, part, landed_ref, codes_ref, stack_ref, swapped_ref):
    half = iota((128, 128), 1) < 64
    blocks = landed_ref[pl.ds(part * 8, 8), parity, pix].reshape(128, 128)
    row = codes_ref[pix, pl.ds(parity * 4 + part, 1), :]
    chooser = jnp.where(slot == row, 1.0, 0.0).astype(bf16)
    turned = pltpu.roll(blocks.astype(f32), 64, 1)
    turned = jnp.where(half, -turned, turned).astype(bf16)
    placed = dot(chooser, jnp.concatenate([blocks, turned], axis=1))
    for q in range(8):
        date = (2 * (8 * part + q) + parity) * 8 + pix
        stack_ref[date] = placed[q * 32 : (q + 1) * 32, :128]
        swapped_ref[date] = placed[q * 32 : (q + 1) * 32, 128:]


def exchange_kernel(
    x_hbm, w_ref, couples_ref, pairs_ref, numbers_ref, places_ref,
    out_ref,
    x_ref, own_codes_ref, c_mid, c_sum, c_all, landed_ref, high_ref, low_ref,
    stack_ref, swapped_ref, phase_ref,
    e_ref, spread_ref, o_ref, z_mid, d_mid, design_ref, left_ref, factor_ref, terms_ref,
    send_z1, recv_z1, send_d1, recv_d1, send_d2, recv_d2, send_z2, recv_z2, local_sem, x_sem,
    send_c1, recv_c1, send_c2, recv_c2,
):
    a = lax.axis_index("date")
    z = lax.axis_index("pix")
    core = lax.rem(a, 2)
    other = 1 - core
    u = lax.div(a, 2)

    def z_of(step):
        return lax.rem(z + step, N_PIX)

    def u_of(step):
        return lax.rem(u + step, HALF_TILES)

    def chunk_of(step):
        return 4 + (1 - 2 * lax.rem(step, 2)) * lax.div(step + 1, 2)

    def load_chunk(step):
        at = lax.rem(lax.div(u, 4) + chunk_of(step), 8)
        rows = pl.ds(pl.multiple_of(at * 1024, 1024), 1024)
        return pltpu.make_async_copy(x_hbm.at[rows], x_ref.at[rows], x_sem.at[step])

    def each(first, last, act):
        def body(step, carry):
            act(step)
            return carry

        lax.fori_loop(first, last, body, 0)

    each(0, 8, lambda s: load_chunk(s).start())

    barrier = pltpu.get_barrier_semaphore()

    def greet(device):
        pl.semaphore_signal(barrier, inc=1, device_id=device, device_id_type=MESH)

    def greet_pix(step, carry):
        greet((a, z_of(step)))
        return carry

    def greet_same(step, carry):
        greet((2 * u_of(step) + core, z))
        return carry

    def greet_other(step, carry):
        greet((2 * u_of(step) + other, z))
        return carry

    lax.fori_loop(1, N_PIX, greet_pix, 0)
    lax.fori_loop(1, HALF_TILES, greet_same, 0)
    lax.fori_loop(0, HALF_TILES, greet_other, 0)

    build_row_matrix(w_ref, e_ref)
    own_code_rows(u, numbers_ref, places_ref, own_codes_ref)

    def remote(src, dst, send, recv, device):
        return pltpu.make_async_remote_copy(
            src_ref=src, dst_ref=dst, send_sem=send, recv_sem=recv,
            device_id=device, device_id_type=MESH,
        )

    row = lax.div(u, 4)

    def pix_first(step):
        to = z_of(step)
        return remote(
            o_ref.at[:, core, to], z_mid.at[z], send_z1.at[0], recv_z1.at[0], (a, to)
        )

    def date_first(step):
        place = lax.div(step, 4)
        x = lax.rem(u + step, 4)
        to = lax.rem(row + place + 2, 8) * 4 + x
        return remote(
            o_ref.at[place * 4 + x, other], d_mid.at[u],
            send_d1.at[0], recv_d1.at[0], (2 * to + other, z),
        )

    def date_second(step):
        place = lax.div(step, 4)
        x = lax.rem(u + step, 4)
        to = lax.rem(row + place + 2, 8) * 4 + x
        return remote(
            z_mid.at[:, place * 4 + x], landed_ref.at[u, core],
            send_d2.at[0], recv_d2.at[lax.div(u, 8)], (2 * to + core, z),
        )

    def pix_second(step):
        to = z_of(step)
        return remote(
            d_mid.at[:, to], landed_ref.at[:, other, z],
            send_z2.at[0], recv_z2.at[step], (a, to),
        )

    def code_first(step, parity):
        to = 2 * u_of(step) + parity
        return remote(
            own_codes_ref.at[to], c_mid.at[a], send_c1.at[0], recv_c1.at[0], (to, z)
        )

    def code_second(step):
        return remote(
            c_sum, c_all.at[z], send_c2.at[0], recv_c2.at[step], (a, z_of(step))
        )

    def arrived(ref, sem):
        remote(ref, ref, sem, sem, (a, z_of(1))).wait_recv()

    def departed(ref, sem):
        remote(ref, ref, sem, sem, (a, z_of(1))).wait_send()

    pick = row_picker()

    def ready_chunk(step):
        down = chunk_of(step)
        place = lax.rem(down + 6, 8)
        load_chunk(step).wait()
        resample_chunk(
            lax.rem(row + down, 8), place, pick, x_ref, e_ref, spread_ref, o_ref
        )

    each(0, 8, ready_chunk)
    pl.semaphore_wait(barrier, N_PIX - 1 + HALF_TILES - 1 + HALF_TILES)
    each(1, N_PIX, lambda s: pix_first(s).start())
    each(0, HALF_TILES, lambda s: date_first(s).start())
    pltpu.make_async_copy(o_ref.at[:, core, z], z_mid.at[z], recv_z1.at[0]).start()
    each(0, HALF_TILES, lambda s: code_first(s, other).start())
    each(1, HALF_TILES, lambda s: code_first(s, core).start())
    pltpu.make_async_copy(own_codes_ref.at[a], c_mid.at[a], recv_c1.at[0]).start()

    parts = normal_parts(couples_ref, design_ref)
    parts = reduce_level(0, parts, left_ref)
    parts = reduce_levels(parts, left_ref, factor_ref, 1, EARLY_LEVELS)

    arrived(c_mid, recv_c1.at[0])
    for e in range(2):
        for p in range(4):
            total = c_mid[16 * p + e]
            for q in range(1, 8):
                total = total + c_mid[16 * p + 2 * q + e]
            c_sum[4 * e + p : 4 * e + p + 1, :] = total
    c_all[z] = c_sum[...]
    each(1, N_PIX, lambda s: code_second(s).start())

    arrived(z_mid, recv_z1.at[0])
    each(0, 24, lambda s: date_second(s).start())
    each(25, 32, lambda s: date_second(s).start())
    pltpu.make_async_copy(
        z_mid.at[:, 24 + lax.rem(u, 4)], landed_ref.at[u, core], recv_d2.at[lax.div(u, 8)]
    ).start()
    arrived(d_mid, recv_d1.at[0])
    each(1, N_PIX, lambda s: pix_second(s).start())
    own_pix = pltpu.make_async_copy(
        d_mid.at[:, z], landed_ref.at[:, other, z], local_sem.at[0]
    )
    own_pix.start()

    parts = reduce_levels(parts, left_ref, factor_ref, EARLY_LEVELS, 6)
    finish_operator(parts, left_ref, factor_ref, terms_ref, design_ref, high_ref, low_ref)

    each(1, N_PIX, lambda s: arrived(c_sum, recv_c2.at[s]))

    line = iota((256, 128), 0)
    column = iota((256, 128), 1)
    fits = (line // 32 == column // 16) & (line // 8 % 4 == column % 4)
    slot = jnp.where(fits, line % 8, -1).astype(f32)

    def place(pix, parity, part):
        place_group(slot, pix, parity, part, landed_ref, c_all, stack_ref, swapped_ref)

    def land_pix(step):
        at = lax.rem(z + N_PIX - step, N_PIX)
        arrived(landed_ref.at[:, other, at], recv_z2.at[step])
        for part in range(4):
            place(at, other, part)

    def land_dates(step):
        part = lax.rem(lax.div(u, 8) + 2 + step, 4)
        arrived(landed_ref.at[pl.ds(part * 8, 8), core], recv_d2.at[part])
        for pix in range(N_PIX):
            place(pix, core, part)

    own_pix.wait()
    for part in range(4):
        place(z, other, part)
    each(1, N_PIX, land_pix)
    each(0, 4, land_dates)

    solve_phases(pairs_ref, high_ref, low_ref, out_ref, stack_ref, swapped_ref, phase_ref)

    departed(own_codes_ref.at[0 : TILES - 1], send_c1.at[0])
    departed(c_all.at[0 : N_PIX - 1], send_c2.at[0])
    departed(o_ref.at[:, 0, 0 : N_PIX - 1], send_z1.at[0])
    departed(o_ref.at[:, 0], send_d1.at[0])
    departed(z_mid.at[:, 0 : HALF_TILES - 1], send_d2.at[0])
    departed(d_mid.at[:, 0 : N_PIX - 1], send_z2.at[0])


def solve_phases(pairs_ref, high_ref, low_ref, out_ref, stack_ref, swapped_ref, phase_ref):
    low_half = iota((8, 128), 1) < 64

    def one_pair(k):
        earlier = stack_ref[pairs_ref[0, k]]
        later = pairs_ref[1, k]
        real = earlier * stack_ref[later]
        imag = earlier * swapped_ref[later]

        def looks(v):
            return (v[0:8] + v[8:16]) + (v[16:24] + v[24:32])

        return looks(real), looks(imag)

    def merge(v, w):
        return jnp.where(low_half, v, w) + pltpu.roll(jnp.where(low_half, w, v), 64, 1)

    def pairs(step, carry):
        found = [
            (one_pair(step * BATCH + q), one_pair(step * BATCH + q + HALF))
            for q in range(BATCH)
        ]
        phases = []
        for (r0, i0), (r1, i1) in found:
            real = merge(r0, r1)
            imag = merge(i0, i1)
            power = jnp.maximum(real * real + imag * imag, float(LOOKS * LOOKS))
            phases.append(imag * lax.rsqrt(power))
        to = pl.ds(pl.multiple_of(step * (8 * BATCH), 8 * BATCH), 8 * BATCH)
        phase_ref[to, :] = jnp.concatenate(phases, axis=0)
        return carry

    lax.fori_loop(0, HALF // BATCH, pairs, 0)

    wide = iota((HALF, 128), 1) < 64
    for part in range(2):
        columns = []
        for p in (2 * part, 2 * part + 1):
            a0 = phase_ref[pl.ds(2 * p, HALF, stride=8), :]
            a1 = phase_ref[pl.ds(2 * p + 1, HALF, stride=8), :]
            columns.append(
                jnp.concatenate(
                    [
                        jnp.where(wide, a0, pltpu.roll(a1, 64, 1)),
                        jnp.where(wide, pltpu.roll(a0, 64, 1), a1),
                    ],
                    axis=0,
                )
            )
        high, low = split2(jnp.concatenate(columns, axis=1))
        out_ref[:, part * 256 : (part + 1) * 256] = dot(high_ref[...], high) + (
            dot(high_ref[...], low) + dot(low_ref[...], high)
        )


def exchange(x, w, couples, numbers, places):
    vmem = pl.BlockSpec(memory_space=pltpu.VMEM)
    smem = pl.BlockSpec(memory_space=pltpu.SMEM)
    dma = pltpu.SemaphoreType.DMA
    return pl.pallas_call(
        exchange_kernel,
        out_shape=jax.ShapeDtypeStruct((DATES, 512), f32),
        in_specs=[pl.BlockSpec(memory_space=pl.ANY), smem, vmem, smem, vmem, vmem],
        out_specs=vmem,
        scratch_shapes=[
            pltpu.VMEM((TILES * 128, 128), bf16),
            pltpu.VMEM((TILES, 1, 128), f32),
            pltpu.VMEM((TILES, 1, 128), f32),
            pltpu.VMEM((8, 128), f32),
            pltpu.VMEM((N_PIX, 8, 128), f32),
            pltpu.VMEM((HALF_TILES, 2, N_PIX, 16, 128), bf16),
            pltpu.VMEM((DATES, PAIRS), bf16),
            pltpu.VMEM((DATES, PAIRS), bf16),
            pltpu.VMEM((DATES, 32, 128), f32),
            pltpu.VMEM((DATES, 32, 128), f32),
            pltpu.VMEM((HALF * 8, 128), f32),
            pltpu.VMEM((512, 512), bf16),
            pltpu.VMEM((CHUNK * 128, 128), f32),
            pltpu.VMEM((HALF_TILES, 2, N_PIX, 16, 128), bf16),
            pltpu.VMEM((N_PIX, HALF_TILES, 16, 128), bf16),
            pltpu.VMEM((HALF_TILES, N_PIX, 16, 128), bf16),
            pltpu.VMEM((DATES, PAIRS), bf16),
            pltpu.VMEM((DATES, DATES), f32),
            pltpu.VMEM((DATES, DATES), f32),
            pltpu.VMEM((3, DATES, DATES), bf16),
            dma((1,)), dma((1,)),
            dma((1,)), dma((1,)),
            dma((1,)), dma((4,)),
            dma((1,)), dma((N_PIX,)),
            dma((1,)), dma((8,)),
            dma((1,)), dma((1,)),
            dma((1,)), dma((N_PIX,)),
        ],
        compiler_params=pltpu.CompilerParams(
            collective_id=0, has_side_effects=True, vmem_limit_bytes=VMEM_BYTES
        ),
        name="exchange",
    )(x, w, couples, couples, numbers, places)


def local(scene_groups, weights, numbers, places, couples):
    return exchange(
        scene_groups.reshape(TILES * 128, 128), weights, couples.T, numbers, places[0].T
    )


def solution(mesh):
    in_specs = (
        P(("date", "pix"), None, None, None, None, None),
        P(("date", "pix"), None),
        P(("date", "pix"), None),
        P(("date", "pix"), None, None),
        P(),
    )
    out_specs = P(None, ("date", "pix"))
    return jax.shard_map(local, mesh=mesh, in_specs=in_specs, out_specs=out_specs, check_vma=False)
```
